128 devices in a mesh: inst: 8 (over y_lo, z), space: 16 (over x, y_hi, core).
Axes of the slice: x: 4, y: 4 (y_hi: 2, y_lo: 2; y = y_hi * 2 + y_lo), z: 4, core: 2. Of those that a mesh axis runs over, the one named last changes fastest.
Arguments:
- velocity: float32 [16, 3, 16, 256, 256], P('inst', None, 'space'), may hold values from -6 to 6
- frequency: float32 [1], replicated, may hold values from 0.6 to 1.4
- slot_time: int32 [16], replicated, may hold values from 0 to 15, each once
- mirror_rows: int32 [256], replicated, may hold values from 0 to 255, as said below
Outputs:
- orbit: float32 [16, 3, 16, 256, 256], P('inst', None, 'space')
- defect: float32 [16, 3, 16, 256, 256], P('inst', None, 'space')
- frequency_new: float32 [1], replicated
The draws below stay inside these ranges and needn't reach their ends.
Inputs may be any that keep to these rules, and one draw needn't show every extreme that they name: `slot_time`: a permutation; slot s lies on index s // 2 of inst. mirror_rows[z] = (256 + c - z) mod 256 for one whole number c of the draw.
All inputs are finite; a program needn't handle non-finite values.
Results may differ from the reference program's by a relative error of at most 0.0001.
Values sent between devices are 32-bit elements; how exact they have to be, the bound alone decides.
A program may use at most 128 MiB of HBM per device.

```python
import jax
import jax.numpy as jnp
from jax import lax

TIMES = 16
NYW = 16
NX = 256
NZ = 256
ITERS = 2


def draw_mirror_rows(key, part):
    key = jax.random.fold_in(key, 7)
    center = jax.random.randint(key, (), 0, NZ)
    return ((center - jnp.arange(NZ)) % NZ).astype(jnp.int32)


def shard_levels(own_key, shape, pieces, low, top_value):
    loudness, own = 1.0, jax.random.fold_in(own_key, 6)
    for position, shards_of in pieces:
        draws = jnp.exp(jax.random.uniform(jax.random.fold_in(own, position), (shards_of,), jnp.float32, low / len(pieces), top_value / len(pieces)))
        loudness = loudness * jnp.repeat(draws, shape[position] // shards_of).reshape([-1 if axis == position else 1 for axis in range(len(shape))])
    return loudness


def noise(own_key, extent, deviation, limit, split=(), kind=jnp.bfloat16):
    entries = jax.random.normal(own_key, extent, jnp.float32) * deviation
    if len(split) > 0:
        entries = shard_levels(own_key, extent, split, -0.22, 0.18) * entries
    return jnp.clip(entries, min=-limit, max=limit).astype(kind)


def setup_inputs(seed: int = 0) -> dict:
    key_of = jax.random.split(jax.random.key(seed), 5)
    velocity = noise(key_of[0], (TIMES, 3, NYW, NX, NZ), 1.0, 6.0, ((0, 8), (2, 16)), jnp.float32)
    frequency = jnp.clip(jax.random.uniform(key_of[1], (1,), jnp.float32, 0.6, 1.4), 0.6, 1.4)
    slot_time = jax.random.permutation(key_of[2], TIMES).astype(jnp.int32)
    mirror_rows = draw_mirror_rows(jax.random.fold_in(key_of[4], 71), 0)
    return {"velocity": velocity, "frequency": frequency, "slot_time": slot_time, "mirror_rows": mirror_rows}


viscosity = 0.5
descent_step = 0.001
frequency_rate = 0.025


def spectral_weights(later, earlier, total):
    gap = (later[:, None] - earlier[None, :]) % total
    angle = jnp.pi * gap.astype(jnp.float32) / total
    parity = 1.0 - 2.0 * (gap % 2).astype(jnp.float32)
    nonzero = gap != 0
    sine = jnp.where(nonzero, jnp.sin(angle), 1.0)
    return jnp.where(nonzero, 0.5 * parity * jnp.cos(angle) / sine, 0.0)


def partner_rows(later, earlier, total):
    return ((later[:, None] + total // 2) % total == earlier[None, :]).astype(jnp.float32)


def reflect_halves(halves, mirror):
    flipped = jnp.take(jnp.flip(halves, axis=-3), mirror, axis=-1)
    sign = jnp.array([1.0, 1.0, -1.0], dtype=halves.dtype).reshape(3, 1, 1, 1, 1)
    return flipped * sign


def reflect(field, mirror):
    shape = field.shape
    halves = field.reshape(shape[:-2] + (2, shape[-2] // 2, shape[-1]))
    return reflect_halves(halves, mirror).reshape(shape)


def spatial_terms(padded, speed):
    center = padded[:, :, 1:-1]
    laplace = (padded[:, :, 2:] + padded[:, :, :-2] + jnp.roll(center, 1, axis=3) + jnp.roll(center, -1, axis=3)
               + jnp.roll(center, 1, axis=4) + jnp.roll(center, -1, axis=4) - 6.0 * center)
    slope = 0.5 * (jnp.roll(center, -1, axis=3) - jnp.roll(center, 1, axis=3))
    return laplace, speed * slope


def apply_time(matrix, field):
    flat = field.reshape(field.shape[0], -1)
    mixed = jnp.dot(matrix, flat, precision=lax.Precision.HIGHEST)
    return mixed.reshape((matrix.shape[0],) + field.shape[1:])


def pad_planes(field):
    return jnp.pad(field, ((0, 0), (0, 0), (1, 1), (0, 0), (0, 0)))


def reference(velocity, frequency, slot_time, mirror_rows):
    total = slot_time.shape[0]
    window = velocity.shape[2]
    plane_ids = jnp.arange(window).astype(jnp.float32)
    speed = (2.0 * (plane_ids + 0.5) / window - 1.0).reshape(window, 1, 1)
    weights_all = spectral_weights(slot_time, slot_time, total)
    partners = partner_rows(slot_time, slot_time, total)
    omega = frequency[0]
    field = velocity
    defect = velocity
    for step in range(ITERS):
        symmetric = 0.5 * (field + reflect(apply_time(partners, field), mirror_rows))
        derivative = apply_time(weights_all, symmetric)
        laplace, advect = spatial_terms(pad_planes(symmetric), speed)
        defect = omega * derivative - viscosity * laplace + advect
        defect_rate = apply_time(weights_all, defect)
        laplace, advect = spatial_terms(pad_planes(defect), speed)
        drift = jnp.sum(defect * derivative) / defect.size
        field = symmetric + descent_step * (omega * defect_rate + viscosity * laplace + advect)
        omega = omega - frequency_rate * drift
    return field, defect, jnp.reshape(omega, (1,))
```

```python
import functools
import math

import jax
import jax.numpy as jnp
from jax import lax
from jax.experimental import pallas as pl
from jax.experimental.pallas import tpu as pltpu
from jax.sharding import PartitionSpec as P

VISCOSITY = 0.5
DESCENT = 0.001
FREQUENCY_RATE = 0.025
MESH = pl.DeviceIdType.MESH
F32 = jnp.float32


def device(x, y, z, core):
    return ((y % 2) * 4 + z, x * 4 + (y // 2) * 2 + core)


def chip_of(j):
    y = j // 4
    r = j % 4
    return y, jnp.where(y % 2 == 0, r, 3 - r)


def weight(k):
    k = k % 16
    if k == 0:
        return 0.0
    angle = math.pi * k / 16
    return 0.5 * (-1.0) ** k * math.cos(angle) / math.sin(angle)


def kernel(
    freq, times, mirror, vel, orbit, defect, fout,
    rbuf0, rbuf1, rbuf2, fld, orb, xsend, xrecv, obuf, mbuf, dbuf, mat, kmat, acc, drift, inv,
    in_send, in_recv, x_send, x_recv, y_send, y_recv, o_send, o_recv, d_send, d_recv,
):
    inst = lax.axis_index("inst")
    space = lax.axis_index("space")
    z = inst % 4
    yhi = space // 2 % 2
    y = yhi * 2 + inst // 4
    x = space // 4
    core = space % 2
    myj = y * 4 + jnp.where(y % 2 == 0, z, 3 - z)
    outs = (defect, orbit)
    rbuf = (rbuf0, rbuf1, rbuf2)

    barrier = pltpu.get_barrier_semaphore()
    place = myj * 2 + core

    def greet_chip(k, carry):
        d = (k + place) % 32
        cy, cz = chip_of(d // 2)
        pl.semaphore_signal(
            barrier, inc=1, device_id=device(x, cy, cz, d % 2), device_id_type=MESH
        )
        return carry

    lax.fori_loop(1, 32, greet_chip, 0)
    for k in range(1, 4):
        pl.semaphore_signal(
            barrier, inc=1, device_id=device((x + k) % 4, y, z, core), device_id_type=MESH
        )
    far = device((x + jnp.where(core == 1, 1, 3)) % 4, y, z, 1 - core)
    near = device(x, y, z, 1 - core)
    pl.semaphore_signal(barrier, inc=1, device_id=far, device_id_type=MESH)

    mat[...] = (
        lax.broadcasted_iota(jnp.int32, (256, 256), 0) == mirror[...]
    ).astype(F32).astype(jnp.bfloat16)
    rows = lax.broadcasted_iota(jnp.int32, (128, 128), 0)
    cols = lax.broadcasted_iota(jnp.int32, (128, 128), 1)
    gap = (rows // 8 - cols // 8 + 16) % 16
    table = jnp.zeros((128, 128), F32)
    for k in range(1, 16):
        table = jnp.where(gap == k, jnp.float32(weight(k)), table)
    kmat[...] = jnp.where(rows % 8 == cols % 8, table, 0.0)

    def invert(t, carry):
        def find(s, found):
            return jnp.where(times[s] == t, s, found)

        inv[t] = lax.fori_loop(0, 16, find, jnp.int32(0))
        return carry

    lax.fori_loop(0, 16, invert, 0)
    bottom = (x == 0) & (core == 0)
    top = (x == 3) & (core == 1)

    @pl.when(bottom)
    def _():
        fld[:, 0] = jnp.zeros((4, 3, 128, 256), F32)

    @pl.when(top)
    def _():
        fld[:, 3] = jnp.zeros((4, 3, 128, 256), F32)

    pl.semaphore_wait(barrier, 35)

    def send_in(c):
        def body(k, carry):
            j = (k + myj) % 16
            cy, cz = chip_of(j)
            di, ds = device(x, cy, cz, yhi)
            src = vel.at[:, c, :, j]
            dst = rbuf[c].at[core, pl.ds(2 * inst, 2)]
            mine = (di == inst) & (ds == space)

            @pl.when(mine)
            def _():
                pltpu.make_async_copy(src, dst, in_recv.at[c]).start()

            @pl.when(jnp.logical_not(mine))
            def _():
                pltpu.make_async_remote_copy(
                    src, dst, in_send, in_recv.at[c], device_id=(di, ds), device_id_type=MESH
                ).start()

            return carry

        lax.fori_loop(0, 16, body, 0)

    for c in range(3):
        send_in(c)

    def reflect_z(v):
        high = v.astype(jnp.bfloat16)
        rest = v - high.astype(F32)
        middle = rest.astype(jnp.bfloat16)
        low = (rest - middle.astype(F32)).astype(jnp.bfloat16)
        m = mat[...]
        parts = [jnp.dot(u, m, preferred_element_type=F32) for u in (high, middle, low)]
        return parts[0] + (parts[1] + parts[2])

    def signed(c, v):
        return -v if c == 2 else v

    left = chip_of((myj + 15) % 16)
    right = chip_of((myj + 1) % 16)

    def send_halo(k, c):
        for p in range(2):
            part = pl.ds(16 * p, 16)
            tiles = fld[k, 1 + p, c].reshape(16, 8, 256)
            xsend[k, 0, c, part] = tiles[:, 0]
            xsend[k, 1, c, part] = tiles[:, 7]
        for side, wraps in ((0, myj == 0), (1, myj == 15)):

            @pl.when(wraps)
            def _():
                turned = signed(c, reflect_z(xsend[k, side, c]))
                for p in range(2):
                    xsend[k, side, c, pl.ds(16 * p, 8)] = turned[16 * p + 8 : 16 * p + 16]
                    xsend[k, side, c, pl.ds(16 * p + 8, 8)] = turned[16 * p : 16 * p + 8]

        for side, (cy, cz) in ((0, left), (1, right)):
            pltpu.make_async_remote_copy(
                xsend.at[k, side, c], xrecv.at[k, 1 - side, c], x_send,
                x_recv.at[k, 1 - side, c], device_id=device(x, cy, cz, core), device_id_type=MESH,
            ).start()

        def planes(up, target):
            src, dst = (2, 0) if up else (1, 3)
            pltpu.make_async_remote_copy(
                fld.at[k, src, c], fld.at[k, dst, c], y_send.at[int(up)],
                y_recv.at[k, int(up), c], device_id=target, device_id_type=MESH,
            ).start()

        @pl.when(core == 0)
        def _():
            planes(True, near)

        @pl.when(core == 1)
        def _():
            planes(False, near)

        @pl.when((core == 1) & (x < 3))
        def _():
            planes(True, far)

        @pl.when((core == 0) & (x > 0))
        def _():
            planes(False, far)

    def wait_for(ref, sem):
        pltpu.make_async_copy(ref, ref, sem).wait()

    def wait_halo(k, c):
        for side in range(2):
            wait_for(xrecv.at[k, side, c], x_recv.at[k, side, c])

        @pl.when(jnp.logical_not(bottom))
        def _():
            wait_for(fld.at[k, 0, c], y_recv.at[k, 1, c])

        @pl.when(jnp.logical_not(top))
        def _():
            wait_for(fld.at[k, 3, c], y_recv.at[k, 0, c])

    row = lax.broadcasted_iota(jnp.int32, (32, 256), 0) % 8

    def spread(v):
        return jnp.broadcast_to(v[:, None, :], (4, 8, 256)).reshape(32, 256)

    def spatial(k, c, p, q):
        part = pl.ds(q * 32, 32)
        v = fld[k, 1 + p, c, part]
        edge = pl.ds(pl.multiple_of(16 * p, 16), 16)
        before = spread(xrecv[k, 0, c, edge][q * 4 : q * 4 + 4])
        after = spread(xrecv[k, 1, c, edge][q * 4 : q * 4 + 4])
        xm = jnp.where(row == 0, before, pltpu.roll(v, 1, 0))
        xp = jnp.where(row == 7, after, pltpu.roll(v, 31, 0))
        total = fld[k, 2 + p, c, part] + fld[k, p, c, part] + xm + xp
        total = total + pltpu.roll(v, 1, 1) + pltpu.roll(v, 255, 1) - 6.0 * v
        plane = (4 * x + 2 * core + p).astype(F32)
        speed = 2.0 * (plane + 0.5) / 16 - 1.0
        return part, total, speed * (0.5 * (xp - xm))

    def derive(k, c):
        for p in range(2):
            dbuf[p] = jnp.dot(
                kmat[...], fld[k, 1 + p, c], preferred_element_type=F32,
                precision=lax.Precision.HIGHEST,
            )

    def symmetrize(c):
        wait_for(rbuf[c], in_recv.at[c])

        def take(p, t, half):
            return rbuf[c][p, inv[t % 16], half]

        for p in range(2):
            other = jnp.concatenate([take(p, t + 8, 1) for t in range(16)], axis=0)
            own = jnp.concatenate([take(p, t, 0) for t in range(16)], axis=0)
            fld[0, 1 + p, c] = 0.5 * (own + signed(c, reflect_z(other)))
        send_halo(0, c)

    def residual(k, c, omega):
        wait_halo(k, c)
        derive(k, c)

        def body(p, carry):
            for q in range(4):
                part, lap, advect = spatial(k, c, p, q)
                d = dbuf[p, part]
                value = omega * d - VISCOSITY * lap + advect
                fld[k + 1, 1 + p, c, part] = value
                acc[k // 2] += value * d
            return carry

        lax.fori_loop(0, 2, body, 0)
        send_halo(k + 1, c)

    def descend(k, c, omega, store):
        wait_halo(k, c)
        derive(k, c)

        def body(p, carry):
            for q in range(4):
                part, lap, advect = spatial(k, c, p, q)
                rate = omega * dbuf[p, part] + VISCOSITY * lap + advect
                store(p, part, fld[k - 1, 1 + p, c, part] + DESCENT * rate)
            return carry

        lax.fori_loop(0, 2, body, 0)

    def next_field(c, omega):
        def store(p, part, value):
            fld[2, 1 + p, c, part] = value

        descend(1, c, omega, store)
        send_halo(2, c)

    stages = (
        (0, 8, z * 2 + core, lambda r: device(x, y, r // 2, r % 2)),
        (8, 4, y, lambda r: device(x, r, z, core)),
        (12, 4, x, lambda r: device(r, y, z, core)),
    )

    def drift_send(it, stage, tile):
        base, size, rank, of = stages[stage]
        drift[it, base + rank] = tile
        for k in range(1, size):
            pltpu.make_async_remote_copy(
                drift.at[it, base + rank], drift.at[it, base + rank], d_send,
                d_recv.at[it, stage], device_id=of((rank + k) % size), device_id_type=MESH,
            ).start()

    def drift_sum(it, stage):
        base, size, _, _ = stages[stage]
        wait_for(drift.at[it, pl.ds(base, size - 1)], d_recv.at[it, stage])
        tile = drift[it, base]
        for k in range(1, size):
            tile = tile + drift[it, base + k]
        return tile

    def drift_start(it):
        a = acc[it]
        tile = a[0:8] + a[8:16] + a[16:24] + a[24:32]
        drift_send(it, 0, tile[:, :128] + tile[:, 128:])

    entries = 16 * 3 * 16 * 256 * 256

    def drift_end(it, omega):
        return omega - FREQUENCY_RATE * (jnp.sum(drift_sum(it, 2)) / (entries // 2))

    def send_out(o, c, source):
        for p in range(2):
            value = source(p)[...]
            turned = signed(c, reflect_z(value)).reshape(16, 8, 256)
            mbuf[p, 0] = value.reshape(16, 8, 256)
            mbuf[p, 1, 0:8] = turned[8:16]
            mbuf[p, 1, 8:16] = turned[0:8]

            def build(s, carry):
                t = times[s]
                at = p * 8 + s // 2
                obuf[o, c, at, s % 2, 0] = mbuf[p, 0, t]
                obuf[o, c, at, s % 2, 1] = mbuf[p, 1, t]
                return carry

            lax.fori_loop(0, 16, build, 0)

        def body(k, carry):
            p = k % 2
            di = (inst + k // 2) % 8
            ds = x * 4 + core * 2 + p
            src = obuf.at[o, c, p * 8 + di]
            dst = outs[o].at[:, c, :, myj]
            mine = (di == inst) & (ds == space)

            @pl.when(mine)
            def _():
                pltpu.make_async_copy(src, dst, o_recv.at[o]).start()

            @pl.when(jnp.logical_not(mine))
            def _():
                pltpu.make_async_remote_copy(
                    src, dst, o_send.at[o], o_recv.at[o], device_id=(di, ds), device_id_type=MESH
                ).start()

            return carry

        lax.fori_loop(0, 16, body, 0)

    acc[...] = jnp.zeros(acc.shape, F32)
    omega = freq[0]
    symmetrize(0)
    residual(0, 0, omega)
    symmetrize(1)
    next_field(0, omega)
    residual(0, 1, omega)
    symmetrize(2)
    next_field(1, omega)
    residual(0, 2, omega)
    drift_start(0)
    next_field(2, omega)
    drift_send(0, 1, drift_sum(0, 0))
    drift_send(0, 2, drift_sum(0, 1))
    omega = drift_end(0, omega)
    for c in range(3):
        residual(2, c, omega)
        send_out(0, c, lambda p: fld.at[3, 1 + p, c])
    drift_start(1)
    for c in range(3):

        def keep(p, part, value):
            orb[p, part] = value

        descend(3, c, omega, keep)
        send_out(1, c, lambda p: orb.at[p])
    drift_send(1, 1, drift_sum(1, 0))
    drift_send(1, 2, drift_sum(1, 1))
    fout[0] = drift_end(1, omega)

    for o in range(2):
        wait_for(outs[o], o_recv.at[o])
    part = pl.ds(0, 15)

    @pl.when(core == yhi)
    def _():
        wait_for(vel.at[:, :, :, part], in_send)
        for o in range(2):
            wait_for(obuf.at[o, :, part], o_send.at[o])

    @pl.when(core != yhi)
    def _():
        wait_for(vel, in_send)
        for o in range(2):
            wait_for(obuf.at[o], o_send.at[o])

    wait_for(xsend, x_send)

    @pl.when(jnp.logical_not(top))
    def _():
        wait_for(fld.at[:, 2], y_send.at[1])

    @pl.when(jnp.logical_not(bottom))
    def _():
        wait_for(fld.at[:, 1], y_send.at[0])

    wait_for(drift.at[:, pl.ds(0, 13)], d_send)


def shards(velocity, frequency, slot_time, mirror_rows):
    cut = (2, 3, 2, 16, 8, 256)
    whole = jax.ShapeDtypeStruct(cut, F32)
    smem = pl.BlockSpec(memory_space=pltpu.SMEM)
    vmem = pl.BlockSpec(memory_space=pltpu.VMEM)
    hbm = pl.BlockSpec(memory_space=pl.ANY)
    dma = pltpu.SemaphoreType.DMA
    orbit, defect, new = pl.pallas_call(
        kernel,
        out_shape=(whole, whole, jax.ShapeDtypeStruct((1,), F32)),
        in_specs=[smem, smem, vmem, hbm],
        out_specs=(hbm, hbm, smem),
        scratch_shapes=[
            pltpu.VMEM((2, 16, 2, 8, 256), F32),
            pltpu.VMEM((2, 16, 2, 8, 256), F32),
            pltpu.VMEM((2, 16, 2, 8, 256), F32),
            pltpu.VMEM((4, 4, 3, 128, 256), F32),
            pltpu.VMEM((2, 128, 256), F32),
            pltpu.VMEM((4, 2, 3, 32, 256), F32),
            pltpu.VMEM((4, 2, 3, 32, 256), F32),
            pltpu.VMEM((2, 3, 16, 2, 2, 8, 256), F32),
            pltpu.VMEM((2, 2, 16, 8, 256), F32),
            pltpu.VMEM((2, 128, 256), F32),
            pltpu.VMEM((256, 256), jnp.bfloat16),
            pltpu.VMEM((128, 128), F32),
            pltpu.VMEM((2, 32, 256), F32),
            pltpu.VMEM((2, 16, 8, 128), F32),
            pltpu.SMEM((16,), jnp.int32),
            dma,
            dma((3,)),
            dma,
            dma((4, 2, 3)),
            dma((2,)),
            dma((4, 2, 3)),
            dma((2,)),
            dma((2,)),
            dma,
            dma((2, 3)),
        ],
        compiler_params=pltpu.CompilerParams(
            collective_id=0, has_side_effects=True, vmem_limit_bytes=40 * 1024 * 1024
        ),
    )(frequency, slot_time, mirror_rows.reshape(1, 256), velocity.reshape(cut))
    return orbit.reshape(velocity.shape), defect.reshape(velocity.shape), new


def solution(mesh):
    spread = P("inst", None, "space", None, None)
    return jax.shard_map(
        shards, mesh=mesh, in_specs=(spread, P(), P(), P()), out_specs=(spread, spread, P()),
        check_vma=False,
    )
```

```python
import functools
import math

import jax
import jax.numpy as jnp
from jax import lax
from jax.experimental import pallas as pl
from jax.experimental.pallas import tpu as pltpu
from jax.sharding import PartitionSpec as P

VISCOSITY = 0.5
DESCENT = 0.001
FREQUENCY_RATE = 0.025
MESH = pl.DeviceIdType.MESH
F32 = jnp.float32


def device(x, y, z, core):
    return ((y % 2) * 4 + z, x * 4 + (y // 2) * 2 + core)


def chip_of(j):
    y = j // 4
    r = j % 4
    return y, jnp.where(y % 2 == 0, r, 3 - r)


def weight(k):
    k = k % 16
    if k == 0:
        return 0.0
    angle = math.pi * k / 16
    return 0.5 * (-1.0) ** k * math.cos(angle) / math.sin(angle)


def kernel(
    freq_in, times_in, mirror_in, vel, orbit, defect, fout, freq, times, mirror,
    rbuf0, rbuf1, rbuf2, fld, orb, xsend, xrecv, obuf, mbuf, dbuf, mat, kmat, acc, drift, inv,
    small, in_send, in_recv, x_send, x_recv, y_send, y_recv, o_send, o_recv, d_send, d_recv,
):
    inst = lax.axis_index("inst")
    space = lax.axis_index("space")
    z = inst % 4
    yhi = space // 2 % 2
    y = yhi * 2 + inst // 4
    x = space // 4
    core = space % 2
    myj = y * 4 + jnp.where(y % 2 == 0, z, 3 - z)
    outs = (defect, orbit)
    rbuf = (rbuf0, rbuf1, rbuf2)

    barrier = pltpu.get_barrier_semaphore()
    place = myj * 2 + core

    def greet_chip(k, carry):
        d = (k + place) % 32
        cy, cz = chip_of(d // 2)
        pl.semaphore_signal(
            barrier, inc=1, device_id=device(x, cy, cz, d % 2), device_id_type=MESH
        )
        return carry

    lax.fori_loop(1, 32, greet_chip, 0)
    for k in range(1, 4):
        pl.semaphore_signal(
            barrier, inc=1, device_id=device((x + k) % 4, y, z, core), device_id_type=MESH
        )
    far = device((x + jnp.where(core == 1, 1, 3)) % 4, y, z, 1 - core)
    near = device(x, y, z, 1 - core)
    pl.semaphore_signal(barrier, inc=1, device_id=far, device_id_type=MESH)

    fetches = [
        pltpu.make_async_copy(src, dst, small.at[k])
        for k, (src, dst) in enumerate(
            ((freq_in, freq), (times_in, times), (mirror_in, mirror))
        )
    ]
    for copy in fetches:
        copy.start()
    pl.semaphore_wait(barrier, 35)

    def send_in(c):
        def body(k, carry):
            j = (k + myj) % 16
            cy, cz = chip_of(j)
            di, ds = device(x, cy, cz, yhi)
            src = vel.at[:, c, :, j]
            dst = rbuf[c].at[core, pl.ds(2 * inst, 2)]
            mine = (di == inst) & (ds == space)

            @pl.when(mine)
            def _():
                pltpu.make_async_copy(src, dst, in_recv.at[c]).start()

            @pl.when(jnp.logical_not(mine))
            def _():
                pltpu.make_async_remote_copy(
                    src, dst, in_send, in_recv.at[c], device_id=(di, ds), device_id_type=MESH
                ).start()

            return carry

        lax.fori_loop(0, 16, body, 0)

    for c in range(3):
        send_in(c)

    for copy in fetches:
        copy.wait()
    mat[...] = (
        lax.broadcasted_iota(jnp.int32, (256, 256), 0) == mirror[...]
    ).astype(F32).astype(jnp.bfloat16)
    rows = lax.broadcasted_iota(jnp.int32, (128, 128), 0)
    cols = lax.broadcasted_iota(jnp.int32, (128, 128), 1)
    gap = (rows // 8 - cols // 8 + 16) % 16
    table = jnp.zeros((128, 128), F32)
    for k in range(1, 16):
        table = jnp.where(gap == k, jnp.float32(weight(k)), table)
    kmat[...] = jnp.where(rows % 8 == cols % 8, table, 0.0)

    def invert(t, carry):
        def find(s, found):
            return jnp.where(times[s] == t, s, found)

        inv[t] = lax.fori_loop(0, 16, find, jnp.int32(0))
        return carry

    lax.fori_loop(0, 16, invert, 0)
    bottom = (x == 0) & (core == 0)
    top = (x == 3) & (core == 1)

    @pl.when(bottom)
    def _():
        fld[:, 0] = jnp.zeros((4, 3, 128, 256), F32)

    @pl.when(top)
    def _():
        fld[:, 3] = jnp.zeros((4, 3, 128, 256), F32)

    def reflect_z(v):
        high = v.astype(jnp.bfloat16)
        rest = v - high.astype(F32)
        middle = rest.astype(jnp.bfloat16)
        low = (rest - middle.astype(F32)).astype(jnp.bfloat16)
        m = mat[...]
        parts = [jnp.dot(u, m, preferred_element_type=F32) for u in (high, middle, low)]
        return parts[0] + (parts[1] + parts[2])

    def signed(c, v):
        return -v if c == 2 else v

    left = chip_of((myj + 15) % 16)
    right = chip_of((myj + 1) % 16)

    def send_halo(k, c):
        for p in range(2):
            part = pl.ds(16 * p, 16)
            tiles = fld[k, 1 + p, c].reshape(16, 8, 256)
            xsend[k, 0, c, part] = tiles[:, 0]
            xsend[k, 1, c, part] = tiles[:, 7]
        for side, wraps in ((0, myj == 0), (1, myj == 15)):

            @pl.when(wraps)
            def _():
                turned = signed(c, reflect_z(xsend[k, side, c]))
                for p in range(2):
                    xsend[k, side, c, pl.ds(16 * p, 8)] = turned[16 * p + 8 : 16 * p + 16]
                    xsend[k, side, c, pl.ds(16 * p + 8, 8)] = turned[16 * p : 16 * p + 8]

        for side, (cy, cz) in ((0, left), (1, right)):
            pltpu.make_async_remote_copy(
                xsend.at[k, side, c], xrecv.at[k, 1 - side, c], x_send,
                x_recv.at[k, 1 - side, c], device_id=device(x, cy, cz, core), device_id_type=MESH,
            ).start()

        def planes(up, target):
            src, dst = (2, 0) if up else (1, 3)
            pltpu.make_async_remote_copy(
                fld.at[k, src, c], fld.at[k, dst, c], y_send.at[int(up)],
                y_recv.at[k, int(up), c], device_id=target, device_id_type=MESH,
            ).start()

        @pl.when(core == 0)
        def _():
            planes(True, near)

        @pl.when(core == 1)
        def _():
            planes(False, near)

        @pl.when((core == 1) & (x < 3))
        def _():
            planes(True, far)

        @pl.when((core == 0) & (x > 0))
        def _():
            planes(False, far)

    def wait_for(ref, sem):
        pltpu.make_async_copy(ref, ref, sem).wait()

    def wait_halo(k, c):
        for side in range(2):
            wait_for(xrecv.at[k, side, c], x_recv.at[k, side, c])

        @pl.when(jnp.logical_not(bottom))
        def _():
            wait_for(fld.at[k, 0, c], y_recv.at[k, 1, c])

        @pl.when(jnp.logical_not(top))
        def _():
            wait_for(fld.at[k, 3, c], y_recv.at[k, 0, c])

    row = lax.broadcasted_iota(jnp.int32, (32, 256), 0) % 8

    def spread(v):
        return jnp.broadcast_to(v[:, None, :], (4, 8, 256)).reshape(32, 256)

    def spatial(k, c, p, q):
        part = pl.ds(q * 32, 32)
        v = fld[k, 1 + p, c, part]
        edge = pl.ds(pl.multiple_of(16 * p, 16), 16)
        before = spread(xrecv[k, 0, c, edge][q * 4 : q * 4 + 4])
        after = spread(xrecv[k, 1, c, edge][q * 4 : q * 4 + 4])
        xm = jnp.where(row == 0, before, pltpu.roll(v, 1, 0))
        xp = jnp.where(row == 7, after, pltpu.roll(v, 31, 0))
        total = fld[k, 2 + p, c, part] + fld[k, p, c, part] + xm + xp
        total = total + pltpu.roll(v, 1, 1) + pltpu.roll(v, 255, 1) - 6.0 * v
        plane = (4 * x + 2 * core + p).astype(F32)
        speed = 2.0 * (plane + 0.5) / 16 - 1.0
        return part, total, speed * (0.5 * (xp - xm))

    def derive(k, c):
        for p in range(2):
            dbuf[p] = jnp.dot(
                kmat[...], fld[k, 1 + p, c], preferred_element_type=F32,
                precision=lax.Precision.HIGHEST,
            )

    def symmetrize(c):
        wait_for(rbuf[c], in_recv.at[c])

        def take(p, t, half):
            return rbuf[c][p, inv[t % 16], half]

        for p in range(2):
            other = jnp.concatenate([take(p, t + 8, 1) for t in range(16)], axis=0)
            own = jnp.concatenate([take(p, t, 0) for t in range(16)], axis=0)
            fld[0, 1 + p, c] = 0.5 * (own + signed(c, reflect_z(other)))
        send_halo(0, c)

    def residual(k, c, omega):
        wait_halo(k, c)
        derive(k, c)

        def body(p, carry):
            for q in range(4):
                part, lap, advect = spatial(k, c, p, q)
                d = dbuf[p, part]
                value = omega * d - VISCOSITY * lap + advect
                fld[k + 1, 1 + p, c, part] = value
                acc[k // 2] += value * d
            return carry

        lax.fori_loop(0, 2, body, 0)
        send_halo(k + 1, c)

    def descend(k, c, omega, store):
        wait_halo(k, c)
        derive(k, c)

        def body(p, carry):
            for q in range(4):
                part, lap, advect = spatial(k, c, p, q)
                rate = omega * dbuf[p, part] + VISCOSITY * lap + advect
                store(p, part, fld[k - 1, 1 + p, c, part] + DESCENT * rate)
            return carry

        lax.fori_loop(0, 2, body, 0)

    def next_field(c, omega):
        def store(p, part, value):
            fld[2, 1 + p, c, part] = value

        descend(1, c, omega, store)
        send_halo(2, c)

    stages = (
        (0, 8, z * 2 + core, lambda r: device(x, y, r // 2, r % 2)),
        (8, 4, y, lambda r: device(x, r, z, core)),
        (12, 4, x, lambda r: device(r, y, z, core)),
    )

    def drift_send(it, stage, tile):
        base, size, rank, of = stages[stage]
        drift[it, base + rank] = tile
        for k in range(1, size):
            pltpu.make_async_remote_copy(
                drift.at[it, base + rank], drift.at[it, base + rank], d_send,
                d_recv.at[it, stage], device_id=of((rank + k) % size), device_id_type=MESH,
            ).start()

    def drift_sum(it, stage):
        base, size, _, _ = stages[stage]
        wait_for(drift.at[it, pl.ds(base, size - 1)], d_recv.at[it, stage])
        tile = drift[it, base]
        for k in range(1, size):
            tile = tile + drift[it, base + k]
        return tile

    def drift_start(it):
        a = acc[it]
        tile = a[0:8] + a[8:16] + a[16:24] + a[24:32]
        drift_send(it, 0, tile[:, :128] + tile[:, 128:])

    entries = 16 * 3 * 16 * 256 * 256

    def drift_end(it, omega):
        return omega - FREQUENCY_RATE * (jnp.sum(drift_sum(it, 2)) / (entries // 2))

    def send_out(o, c, source):
        for p in range(2):
            value = source(p)[...]
            turned = signed(c, reflect_z(value)).reshape(16, 8, 256)
            mbuf[p, 0] = value.reshape(16, 8, 256)
            mbuf[p, 1, 0:8] = turned[8:16]
            mbuf[p, 1, 8:16] = turned[0:8]

            def build(s, carry):
                t = times[s]
                at = p * 8 + s // 2
                obuf[o, c, at, s % 2, 0] = mbuf[p, 0, t]
                obuf[o, c, at, s % 2, 1] = mbuf[p, 1, t]
                return carry

            lax.fori_loop(0, 16, build, 0)

        def body(k, carry):
            p = k % 2
            di = (inst + k // 2) % 8
            ds = x * 4 + core * 2 + p
            src = obuf.at[o, c, p * 8 + di]
            dst = outs[o].at[:, c, :, myj]
            mine = (di == inst) & (ds == space)

            @pl.when(mine)
            def _():
                pltpu.make_async_copy(src, dst, o_recv.at[o]).start()

            @pl.when(jnp.logical_not(mine))
            def _():
                pltpu.make_async_remote_copy(
                    src, dst, o_send.at[o], o_recv.at[o], device_id=(di, ds), device_id_type=MESH
                ).start()

            return carry

        lax.fori_loop(0, 16, body, 0)

    acc[...] = jnp.zeros(acc.shape, F32)
    omega = freq[0]
    for c in range(3):
        symmetrize(c)
    for c in range(3):
        residual(0, c, omega)
    drift_start(0)
    next_field(0, omega)
    drift_send(0, 1, drift_sum(0, 0))
    next_field(1, omega)
    drift_send(0, 2, drift_sum(0, 1))
    next_field(2, omega)
    omega = drift_end(0, omega)
    for c in range(3):
        residual(2, c, omega)
        send_out(0, c, lambda p: fld.at[3, 1 + p, c])
    drift_start(1)
    for c in range(3):

        def keep(p, part, value):
            orb[p, part] = value

        descend(3, c, omega, keep)
        send_out(1, c, lambda p: orb.at[p])
    drift_send(1, 1, drift_sum(1, 0))
    drift_send(1, 2, drift_sum(1, 1))
    freq[0] = drift_end(1, omega)
    result = pltpu.make_async_copy(freq, fout, small.at[0])
    result.start()
    result.wait()

    for o in range(2):
        wait_for(outs[o], o_recv.at[o])
    part = pl.ds(0, 15)

    @pl.when(core == yhi)
    def _():
        wait_for(vel.at[:, :, :, part], in_send)
        for o in range(2):
            wait_for(obuf.at[o, :, part], o_send.at[o])

    @pl.when(core != yhi)
    def _():
        wait_for(vel, in_send)
        for o in range(2):
            wait_for(obuf.at[o], o_send.at[o])

    wait_for(xsend, x_send)

    @pl.when(jnp.logical_not(top))
    def _():
        wait_for(fld.at[:, 2], y_send.at[1])

    @pl.when(jnp.logical_not(bottom))
    def _():
        wait_for(fld.at[:, 1], y_send.at[0])

    wait_for(drift.at[:, pl.ds(0, 13)], d_send)


def finish(orbit, defect, new, orbit_out, defect_out, new_out, one, sems):
    first = pltpu.make_async_copy(new, one, sems.at[0])
    first.start()
    copies = [
        pltpu.make_async_copy(src.at[s], dst.at[s], sems.at[1 + 2 * k + s])
        for k, (src, dst) in enumerate(((orbit, orbit_out), (defect, defect_out)))
        for s in range(2)
    ]
    for copy in copies:
        copy.start()
    first.wait()
    copies.append(pltpu.make_async_copy(one, new_out, sems.at[5]))
    copies[-1].start()
    for copy in copies:
        copy.wait()


def shards(velocity, frequency, slot_time, mirror_rows):
    cut = (2, 3, 2, 16, 8, 256)
    whole = jax.ShapeDtypeStruct(cut, F32)
    shapes = (whole, whole, jax.ShapeDtypeStruct((1,), F32))
    hbm = pl.BlockSpec(memory_space=pltpu.HBM)
    vmem = pl.BlockSpec(memory_space=pltpu.VMEM)
    dma = pltpu.SemaphoreType.DMA
    results = pl.pallas_call(
        kernel,
        out_shape=(pltpu.VMEM(cut, F32), pltpu.VMEM(cut, F32), shapes[2]),
        in_specs=[hbm] * 4,
        out_specs=(vmem, vmem, hbm),
        scratch_shapes=[
            pltpu.SMEM((1,), F32),
            pltpu.SMEM((16,), jnp.int32),
            pltpu.VMEM((1, 256), jnp.int32),
            pltpu.VMEM((2, 16, 2, 8, 256), F32),
            pltpu.VMEM((2, 16, 2, 8, 256), F32),
            pltpu.VMEM((2, 16, 2, 8, 256), F32),
            pltpu.VMEM((4, 4, 3, 128, 256), F32),
            pltpu.VMEM((2, 128, 256), F32),
            pltpu.VMEM((4, 2, 3, 32, 256), F32),
            pltpu.VMEM((4, 2, 3, 32, 256), F32),
            pltpu.VMEM((2, 3, 16, 2, 2, 8, 256), F32),
            pltpu.VMEM((2, 2, 16, 8, 256), F32),
            pltpu.VMEM((2, 128, 256), F32),
            pltpu.VMEM((256, 256), jnp.bfloat16),
            pltpu.VMEM((128, 128), F32),
            pltpu.VMEM((2, 32, 256), F32),
            pltpu.VMEM((2, 16, 8, 128), F32),
            pltpu.SMEM((16,), jnp.int32),
            dma((3,)),
            dma,
            dma((3,)),
            dma,
            dma((4, 2, 3)),
            dma((2,)),
            dma((4, 2, 3)),
            dma((2,)),
            dma((2,)),
            dma,
            dma((2, 3)),
        ],
        compiler_params=pltpu.CompilerParams(
            collective_id=0, has_side_effects=True, vmem_limit_bytes=40 * 1024 * 1024
        ),
    )(frequency, *[
        pltpu.with_memory_space_constraint(v, pltpu.HBM)
        for v in (slot_time, mirror_rows.reshape(1, 256), velocity.reshape(cut))
    ])
    orbit, defect, new = pl.pallas_call(
        finish,
        out_shape=shapes,
        in_specs=[vmem, vmem, hbm],
        out_specs=(hbm,) * 3,
        scratch_shapes=[pltpu.SMEM((1,), F32), dma((6,))],
        compiler_params=pltpu.CompilerParams(vmem_limit_bytes=4 * 1024 * 1024),
    )(*results)
    return orbit.reshape(velocity.shape), defect.reshape(velocity.shape), new


def solution(mesh):
    spread = P("inst", None, "space", None, None)
    return jax.shard_map(
        shards, mesh=mesh, in_specs=(spread, P(), P(), P()), out_specs=(spread, spread, P()),
        check_vma=False,
    )
```

```python
import functools
import math

import jax
import jax.numpy as jnp
from jax import lax
from jax.experimental import pallas as pl
from jax.experimental.pallas import tpu as pltpu
from jax.sharding import PartitionSpec as P

VISCOSITY = 0.5
DESCENT = 0.001
FREQUENCY_RATE = 0.025
MESH = pl.DeviceIdType.MESH
F32 = jnp.float32


def device(x, y, z, core):
    return ((y % 2) * 4 + z, x * 4 + (y // 2) * 2 + core)


def chip_of(j):
    y = j // 4
    r = j % 4
    return y, jnp.where(y % 2 == 0, r, 3 - r)


def weight(k):
    k = k % 16
    if k == 0:
        return 0.0
    angle = math.pi * k / 16
    return 0.5 * (-1.0) ** k * math.cos(angle) / math.sin(angle)


def kernel(
    freq_in, times_in, mirror_in, vel, orbit, defect, fout, freq, times, mirror,
    rbuf0, rbuf1, rbuf2, fld, orb, xsend, xrecv, obuf, mbuf, dbuf, mat, kmat, acc, drift, inv,
    small, in_send, in_recv, x_send, x_recv, y_send, y_recv, o_send, o_recv, d_send, d_recv,
):
    inst = lax.axis_index("inst")
    space = lax.axis_index("space")
    z = inst % 4
    yhi = space // 2 % 2
    y = yhi * 2 + inst // 4
    x = space // 4
    core = space % 2
    myj = y * 4 + jnp.where(y % 2 == 0, z, 3 - z)
    outs = (defect, orbit)
    rbuf = (rbuf0, rbuf1, rbuf2)

    barrier = pltpu.get_barrier_semaphore()
    place = myj * 2 + core

    def greet_chip(k, carry):
        d = (k + place) % 32
        cy, cz = chip_of(d // 2)
        pl.semaphore_signal(
            barrier, inc=1, device_id=device(x, cy, cz, d % 2), device_id_type=MESH
        )
        return carry

    lax.fori_loop(1, 32, greet_chip, 0)

    def greet_plane(k, carry):
        dx = (x + 1 + k // 4) % 4
        pl.semaphore_signal(
            barrier, inc=1, device_id=device(dx, (y + k) % 4, z, core), device_id_type=MESH
        )
        return carry

    lax.fori_loop(0, 12, greet_plane, 0)
    far = device((x + jnp.where(core == 1, 1, 3)) % 4, y, z, 1 - core)
    near = device(x, y, z, 1 - core)
    pl.semaphore_signal(barrier, inc=1, device_id=far, device_id_type=MESH)

    fetches = [
        pltpu.make_async_copy(src, dst, small.at[k])
        for k, (src, dst) in enumerate(
            ((freq_in, freq), (times_in, times), (mirror_in, mirror))
        )
    ]
    for copy in fetches:
        copy.start()
    pl.semaphore_wait(barrier, 44)

    def send_in(c):
        def body(k, carry):
            j = (k + myj) % 16
            cy, cz = chip_of(j)
            di, ds = device(x, cy, cz, yhi)
            src = vel.at[:, c, :, j]
            dst = rbuf[c].at[core, pl.ds(2 * inst, 2)]
            mine = (di == inst) & (ds == space)

            @pl.when(mine)
            def _():
                pltpu.make_async_copy(src, dst, in_recv.at[c]).start()

            @pl.when(jnp.logical_not(mine))
            def _():
                pltpu.make_async_remote_copy(
                    src, dst, in_send, in_recv.at[c], device_id=(di, ds), device_id_type=MESH
                ).start()

            return carry

        lax.fori_loop(0, 16, body, 0)

    for c in range(3):
        send_in(c)

    for copy in fetches:
        copy.wait()
    mat[...] = (
        lax.broadcasted_iota(jnp.int32, (256, 256), 0) == mirror[...]
    ).astype(F32).astype(jnp.bfloat16)
    rows = lax.broadcasted_iota(jnp.int32, (128, 128), 0)
    cols = lax.broadcasted_iota(jnp.int32, (128, 128), 1)
    gap = (rows // 8 - cols // 8 + 16) % 16
    table = jnp.zeros((128, 128), F32)
    for k in range(1, 16):
        table = jnp.where(gap == k, jnp.float32(weight(k)), table)
    kmat[...] = jnp.where(rows % 8 == cols % 8, table, 0.0)

    def invert(t, carry):
        def find(s, found):
            return jnp.where(times[s] == t, s, found)

        inv[t] = lax.fori_loop(0, 16, find, jnp.int32(0))
        return carry

    lax.fori_loop(0, 16, invert, 0)
    bottom = (x == 0) & (core == 0)
    top = (x == 3) & (core == 1)

    @pl.when(bottom)
    def _():
        fld[:, 0] = jnp.zeros((4, 3, 128, 256), F32)

    @pl.when(top)
    def _():
        fld[:, 3] = jnp.zeros((4, 3, 128, 256), F32)

    def reflect_z(v):
        high = v.astype(jnp.bfloat16)
        rest = v - high.astype(F32)
        middle = rest.astype(jnp.bfloat16)
        low = (rest - middle.astype(F32)).astype(jnp.bfloat16)
        m = mat[...]
        parts = [jnp.dot(u, m, preferred_element_type=F32) for u in (high, middle, low)]
        return parts[0] + (parts[1] + parts[2])

    def signed(c, v):
        return -v if c == 2 else v

    left = chip_of((myj + 15) % 16)
    right = chip_of((myj + 1) % 16)

    def send_halo(k, c):
        for p in range(2):
            part = pl.ds(16 * p, 16)
            tiles = fld[k, 1 + p, c].reshape(16, 8, 256)
            xsend[k, 0, c, part] = tiles[:, 0]
            xsend[k, 1, c, part] = tiles[:, 7]
        for side, wraps in ((0, myj == 0), (1, myj == 15)):

            @pl.when(wraps)
            def _():
                turned = signed(c, reflect_z(xsend[k, side, c]))
                for p in range(2):
                    xsend[k, side, c, pl.ds(16 * p, 8)] = turned[16 * p + 8 : 16 * p + 16]
                    xsend[k, side, c, pl.ds(16 * p + 8, 8)] = turned[16 * p : 16 * p + 8]

        for side, (cy, cz) in ((0, left), (1, right)):
            pltpu.make_async_remote_copy(
                xsend.at[k, side, c], xrecv.at[k, 1 - side, c], x_send,
                x_recv.at[k, 1 - side, c], device_id=device(x, cy, cz, core), device_id_type=MESH,
            ).start()

        def planes(up, target):
            src, dst = (2, 0) if up else (1, 3)
            pltpu.make_async_remote_copy(
                fld.at[k, src, c], fld.at[k, dst, c], y_send.at[int(up)],
                y_recv.at[k, int(up), c], device_id=target, device_id_type=MESH,
            ).start()

        @pl.when(core == 0)
        def _():
            planes(True, near)

        @pl.when(core == 1)
        def _():
            planes(False, near)

        @pl.when((core == 1) & (x < 3))
        def _():
            planes(True, far)

        @pl.when((core == 0) & (x > 0))
        def _():
            planes(False, far)

    def wait_for(ref, sem):
        pltpu.make_async_copy(ref, ref, sem).wait()

    def wait_halo(k, c):
        for side in range(2):
            wait_for(xrecv.at[k, side, c], x_recv.at[k, side, c])

        @pl.when(jnp.logical_not(bottom))
        def _():
            wait_for(fld.at[k, 0, c], y_recv.at[k, 1, c])

        @pl.when(jnp.logical_not(top))
        def _():
            wait_for(fld.at[k, 3, c], y_recv.at[k, 0, c])

    row = lax.broadcasted_iota(jnp.int32, (32, 256), 0) % 8

    def spread(v):
        return jnp.broadcast_to(v[:, None, :], (4, 8, 256)).reshape(32, 256)

    def spatial(k, c, p, q):
        part = pl.ds(q * 32, 32)
        v = fld[k, 1 + p, c, part]
        edge = pl.ds(pl.multiple_of(16 * p, 16), 16)
        before = spread(xrecv[k, 0, c, edge][q * 4 : q * 4 + 4])
        after = spread(xrecv[k, 1, c, edge][q * 4 : q * 4 + 4])
        xm = jnp.where(row == 0, before, pltpu.roll(v, 1, 0))
        xp = jnp.where(row == 7, after, pltpu.roll(v, 31, 0))
        total = fld[k, 2 + p, c, part] + fld[k, p, c, part] + xm + xp
        total = total + pltpu.roll(v, 1, 1) + pltpu.roll(v, 255, 1) - 6.0 * v
        plane = (4 * x + 2 * core + p).astype(F32)
        speed = 2.0 * (plane + 0.5) / 16 - 1.0
        return part, total, speed * (0.5 * (xp - xm))

    def derive(k, c):
        for p in range(2):
            dbuf[c, p] = jnp.dot(
                kmat[...], fld[k, 1 + p, c], preferred_element_type=F32,
                precision=lax.Precision.HIGHEST,
            )

    def symmetrize(c):
        wait_for(rbuf[c], in_recv.at[c])

        def take(p, t, half):
            return rbuf[c][p, inv[t % 16], half]

        for p in range(2):
            other = jnp.concatenate([take(p, t + 8, 1) for t in range(16)], axis=0)
            own = jnp.concatenate([take(p, t, 0) for t in range(16)], axis=0)
            fld[0, 1 + p, c] = 0.5 * (own + signed(c, reflect_z(other)))
        send_halo(0, c)

    def residual(c, omega):
        wait_halo(0, c)
        derive(0, c)

        def body(p, carry):
            for q in range(4):
                part, lap, advect = spatial(0, c, p, q)
                d = dbuf[c, p, part]
                value = omega * d - VISCOSITY * lap + advect
                fld[1, 1 + p, c, part] = value
                acc[0] += value * d
            return carry

        lax.fori_loop(0, 2, body, 0)

    def prepare(c):
        wait_halo(2, c)
        derive(2, c)

        def body(p, carry):
            for q in range(4):
                part, lap, advect = spatial(2, c, p, q)
                fld[3, 1 + p, c, part] = advect - VISCOSITY * lap
            return carry

        lax.fori_loop(0, 2, body, 0)

    def complete(c, omega):
        def body(p, carry):
            for q in range(4):
                part = pl.ds(q * 32, 32)
                d = dbuf[c, p, part]
                value = omega * d + fld[3, 1 + p, c, part]
                fld[3, 1 + p, c, part] = value
                acc[1] += value * d
            return carry

        lax.fori_loop(0, 2, body, 0)
        send_halo(3, c)

    def descend(k, c, omega, store):
        wait_halo(k, c)
        derive(k, c)

        def body(p, carry):
            for q in range(4):
                part, lap, advect = spatial(k, c, p, q)
                rate = omega * dbuf[c, p, part] + VISCOSITY * lap + advect
                store(p, part, fld[k - 1, 1 + p, c, part] + DESCENT * rate)
            return carry

        lax.fori_loop(0, 2, body, 0)

    def next_field(c, omega):
        def store(p, part, value):
            fld[2, 1 + p, c, part] = value

        descend(1, c, omega, store)
        send_halo(2, c)

    stages = (
        (0, 8, z * 2 + core, lambda r: device(x, y, r // 2, r % 2)),
        (8, 16, x * 4 + y, lambda r: device(r // 4, r % 4, z, core)),
    )

    def drift_send(it, stage, tile):
        base, size, rank, of = stages[stage]
        drift[it, base + rank] = tile

        def body(k, carry):
            pltpu.make_async_remote_copy(
                drift.at[it, base + rank], drift.at[it, base + rank], d_send,
                d_recv.at[it, stage], device_id=of((rank + k) % size), device_id_type=MESH,
            ).start()
            return carry

        lax.fori_loop(1, size, body, 0)

    def drift_sum(it, stage):
        base, size, _, _ = stages[stage]
        wait_for(drift.at[it, pl.ds(base, size - 1)], d_recv.at[it, stage])
        tile = drift[it, base]
        for k in range(1, size):
            tile = tile + drift[it, base + k]
        return tile

    def drift_start(it):
        a = acc[it]
        tile = a[0:8] + a[8:16] + a[16:24] + a[24:32]
        drift_send(it, 0, tile[:, :128] + tile[:, 128:])

    entries = 16 * 3 * 16 * 256 * 256

    def drift_end(it, omega):
        return omega - FREQUENCY_RATE * (jnp.sum(drift_sum(it, 1)) / (entries // 2))

    def send_out(o, c, source):
        for p in range(2):
            value = source(p)[...]
            turned = signed(c, reflect_z(value)).reshape(16, 8, 256)
            mbuf[p, 0] = value.reshape(16, 8, 256)
            mbuf[p, 1, 0:8] = turned[8:16]
            mbuf[p, 1, 8:16] = turned[0:8]

            def build(i, carry):
                for s in range(2):
                    t = times[2 * i + s]
                    obuf[o, c, p * 8 + i, s, 0] = mbuf[p, 0, t]
                    obuf[o, c, p * 8 + i, s, 1] = mbuf[p, 1, t]
                return carry

            lax.fori_loop(0, 8, build, 0)

            def body(k, carry):
                di = (inst + k) % 8
                ds = x * 4 + core * 2 + p
                src = obuf.at[o, c, p * 8 + di]
                dst = outs[o].at[:, c, :, myj]
                mine = (di == inst) & (ds == space)

                @pl.when(mine)
                def _():
                    pltpu.make_async_copy(src, dst, o_recv.at[o]).start()

                @pl.when(jnp.logical_not(mine))
                def _():
                    pltpu.make_async_remote_copy(
                        src, dst, o_send.at[o], o_recv.at[o], device_id=(di, ds),
                        device_id_type=MESH,
                    ).start()

                return carry

            lax.fori_loop(0, 8, body, 0)

    acc[...] = jnp.zeros(acc.shape, F32)
    omega = freq[0]
    for c in range(3):
        symmetrize(c)
    for c in range(3):
        residual(c, omega)
        if c == 2:
            drift_start(0)
        send_halo(1, c)
    next_field(0, omega)
    drift_send(0, 1, drift_sum(0, 0))
    next_field(1, omega)
    next_field(2, omega)
    prepare(0)
    omega = drift_end(0, omega)
    for c in range(3):
        if c > 0:
            prepare(c)
        complete(c, omega)
        if c == 2:
            drift_start(1)
        send_out(0, c, lambda p: fld.at[3, 1 + p, c])
    for c in range(3):

        def keep(p, part, value):
            orb[p, part] = value

        descend(3, c, omega, keep)
        if c == 0:
            drift_send(1, 1, drift_sum(1, 0))
        send_out(1, c, lambda p: orb.at[p])
    freq[0] = drift_end(1, omega)
    result = pltpu.make_async_copy(freq, fout, small.at[0])
    result.start()
    result.wait()

    for o in range(2):
        wait_for(outs[o], o_recv.at[o])
    part = pl.ds(0, 15)

    @pl.when(core == yhi)
    def _():
        wait_for(vel.at[:, :, :, part], in_send)
        for o in range(2):
            wait_for(obuf.at[o, :, part], o_send.at[o])

    @pl.when(core != yhi)
    def _():
        wait_for(vel, in_send)
        for o in range(2):
            wait_for(obuf.at[o], o_send.at[o])

    wait_for(xsend, x_send)

    @pl.when(jnp.logical_not(top))
    def _():
        wait_for(fld.at[:, 2], y_send.at[1])

    @pl.when(jnp.logical_not(bottom))
    def _():
        wait_for(fld.at[:, 1], y_send.at[0])

    wait_for(drift.at[:, pl.ds(0, 22)], d_send)


def finish(orbit, defect, new, orbit_out, defect_out, new_out, one, sems):
    first = pltpu.make_async_copy(new, one, sems.at[0])
    first.start()
    copies = [
        pltpu.make_async_copy(src.at[s], dst.at[s], sems.at[1 + 2 * k + s])
        for k, (src, dst) in enumerate(((orbit, orbit_out), (defect, defect_out)))
        for s in range(2)
    ]
    for copy in copies:
        copy.start()
    first.wait()
    copies.append(pltpu.make_async_copy(one, new_out, sems.at[5]))
    copies[-1].start()
    for copy in copies:
        copy.wait()


def shards(velocity, frequency, slot_time, mirror_rows):
    cut = (2, 3, 2, 16, 8, 256)
    whole = jax.ShapeDtypeStruct(cut, F32)
    shapes = (whole, whole, jax.ShapeDtypeStruct((1,), F32))
    hbm = pl.BlockSpec(memory_space=pltpu.HBM)
    vmem = pl.BlockSpec(memory_space=pltpu.VMEM)
    dma = pltpu.SemaphoreType.DMA
    results = pl.pallas_call(
        kernel,
        out_shape=(pltpu.VMEM(cut, F32), pltpu.VMEM(cut, F32), shapes[2]),
        in_specs=[hbm] * 4,
        out_specs=(vmem, vmem, hbm),
        scratch_shapes=[
            pltpu.SMEM((1,), F32),
            pltpu.SMEM((16,), jnp.int32),
            pltpu.VMEM((1, 256), jnp.int32),
            pltpu.VMEM((2, 16, 2, 8, 256), F32),
            pltpu.VMEM((2, 16, 2, 8, 256), F32),
            pltpu.VMEM((2, 16, 2, 8, 256), F32),
            pltpu.VMEM((4, 4, 3, 128, 256), F32),
            pltpu.VMEM((2, 128, 256), F32),
            pltpu.VMEM((4, 2, 3, 32, 256), F32),
            pltpu.VMEM((4, 2, 3, 32, 256), F32),
            pltpu.VMEM((2, 3, 16, 2, 2, 8, 256), F32),
            pltpu.VMEM((2, 2, 16, 8, 256), F32),
            pltpu.VMEM((3, 2, 128, 256), F32),
            pltpu.VMEM((256, 256), jnp.bfloat16),
            pltpu.VMEM((128, 128), F32),
            pltpu.VMEM((2, 32, 256), F32),
            pltpu.VMEM((2, 24, 8, 128), F32),
            pltpu.SMEM((16,), jnp.int32),
            dma((3,)),
            dma,
            dma((3,)),
            dma,
            dma((4, 2, 3)),
            dma((2,)),
            dma((4, 2, 3)),
            dma((2,)),
            dma((2,)),
            dma,
            dma((2, 2)),
        ],
        compiler_params=pltpu.CompilerParams(
            collective_id=0, has_side_effects=True, vmem_limit_bytes=40 * 1024 * 1024
        ),
    )(frequency, *[
        pltpu.with_memory_space_constraint(v, pltpu.HBM)
        for v in (slot_time, mirror_rows.reshape(1, 256), velocity.reshape(cut))
    ])
    orbit, defect, new = pl.pallas_call(
        finish,
        out_shape=shapes,
        in_specs=[vmem, vmem, hbm],
        out_specs=(hbm,) * 3,
        scratch_shapes=[pltpu.SMEM((1,), F32), dma((6,))],
        compiler_params=pltpu.CompilerParams(vmem_limit_bytes=4 * 1024 * 1024),
    )(*results)
    return orbit.reshape(velocity.shape), defect.reshape(velocity.shape), new


def solution(mesh):
    spread = P("inst", None, "space", None, None)
    return jax.shard_map(
        shards, mesh=mesh, in_specs=(spread, P(), P(), P()), out_specs=(spread, spread, P()),
        check_vma=False,
    )
```

```python
import functools
import math

import jax
import jax.numpy as jnp
from jax import lax
from jax.experimental import pallas as pl
from jax.experimental.pallas import tpu as pltpu
from jax.sharding import PartitionSpec as P

VISCOSITY = 0.5
DESCENT = 0.001
FREQUENCY_RATE = 0.025
MESH = pl.DeviceIdType.MESH
F32 = jnp.float32


def device(x, y, z, core):
    return ((y % 2) * 4 + z, x * 4 + (y // 2) * 2 + core)


def chip_of(j):
    y = j // 4
    r = j % 4
    return y, jnp.where(y % 2 == 0, r, 3 - r)


def weight(k):
    k = k % 16
    if k == 0:
        return 0.0
    angle = math.pi * k / 16
    return 0.5 * (-1.0) ** k * math.cos(angle) / math.sin(angle)


def kernel(
    freq_in, times_in, mirror_in, vel, orbit, defect, fout, freq, times, mirror,
    rbuf0, rbuf1, rbuf2, fld, orb, xsend, xrecv, obuf, mbuf, dbuf, mat, kmat, acc, drift, inv,
    small, in_send, in_recv, x_send, x_recv, y_send, y_recv, o_send, o_recv, d_send, d_recv,
):
    inst = lax.axis_index("inst")
    space = lax.axis_index("space")
    z = inst % 4
    yhi = space // 2 % 2
    y = yhi * 2 + inst // 4
    x = space // 4
    core = space % 2
    myj = y * 4 + jnp.where(y % 2 == 0, z, 3 - z)
    outs = (defect, orbit)
    rbuf = (rbuf0, rbuf1, rbuf2)

    barrier = pltpu.get_barrier_semaphore()

    steps = sorted(
        ((dy, dz, dc) for dy in range(4) for dz in range(4) for dc in range(2)),
        key=lambda d: -min(d[0], 4 - d[0]) - min(d[1], 4 - d[1]),
    )
    friends = [
        device(x, (y + dy) % 4, (z + dz) % 4, (core + dc) % 2)
        for dy, dz, dc in steps if dy + dz > 0
    ]
    friends += [device((x + 1 + k // 2) % 4, y, z, (core + k) % 2) for k in (2, 3, 0, 1, 4, 5)]
    friends += [device(x, y, z, 1 - core)]
    for friend in friends:
        pl.semaphore_signal(barrier, inc=1, device_id=friend, device_id_type=MESH)
    far = device((x + jnp.where(core == 1, 1, 3)) % 4, y, z, 1 - core)
    near = device(x, y, z, 1 - core)
    fetches = [
        pltpu.make_async_copy(src, dst, small.at[k])
        for k, (src, dst) in enumerate(
            ((freq_in, freq), (times_in, times), (mirror_in, mirror))
        )
    ]
    for copy in fetches:
        copy.start()
    pl.semaphore_wait(barrier, len(friends))

    def send_in(c):
        def body(k, carry):
            j = (k + myj) % 16
            cy, cz = chip_of(j)
            di, ds = device(x, cy, cz, yhi)
            src = vel.at[:, c, :, j]
            dst = rbuf[c].at[core, pl.ds(2 * inst, 2)]
            mine = (di == inst) & (ds == space)

            @pl.when(mine)
            def _():
                pltpu.make_async_copy(src, dst, in_recv.at[c]).start()

            @pl.when(jnp.logical_not(mine))
            def _():
                pltpu.make_async_remote_copy(
                    src, dst, in_send, in_recv.at[c], device_id=(di, ds), device_id_type=MESH
                ).start()

            return carry

        lax.fori_loop(0, 16, body, 0)

    for c in range(3):
        send_in(c)

    for copy in fetches:
        copy.wait()
    mat[...] = (
        lax.broadcasted_iota(jnp.int32, (256, 256), 0) == mirror[...]
    ).astype(F32).astype(jnp.bfloat16)
    rows = lax.broadcasted_iota(jnp.int32, (128, 128), 0)
    cols = lax.broadcasted_iota(jnp.int32, (128, 128), 1)
    gap = (rows // 8 - cols // 8 + 16) % 16
    table = jnp.zeros((128, 128), F32)
    for k in range(1, 16):
        table = jnp.where(gap == k, jnp.float32(weight(k)), table)
    kmat[...] = jnp.where(rows % 8 == cols % 8, table, 0.0)

    def invert(t, carry):
        def find(s, found):
            return jnp.where(times[s] == t, s, found)

        inv[t] = lax.fori_loop(0, 16, find, jnp.int32(0))
        return carry

    lax.fori_loop(0, 16, invert, 0)
    bottom = (x == 0) & (core == 0)
    top = (x == 3) & (core == 1)

    @pl.when(bottom)
    def _():
        fld[:, 0] = jnp.zeros((4, 3, 128, 256), F32)

    @pl.when(top)
    def _():
        fld[:, 3] = jnp.zeros((4, 3, 128, 256), F32)

    def reflect_z(v):
        high = v.astype(jnp.bfloat16)
        rest = v - high.astype(F32)
        middle = rest.astype(jnp.bfloat16)
        low = (rest - middle.astype(F32)).astype(jnp.bfloat16)
        m = mat[...]
        parts = [jnp.dot(u, m, preferred_element_type=F32) for u in (high, middle, low)]
        return parts[0] + (parts[1] + parts[2])

    def signed(c, v):
        return -v if c == 2 else v

    left = chip_of((myj + 15) % 16)
    right = chip_of((myj + 1) % 16)

    def send_halo(k, c):
        def planes(up, target):
            src, dst = (2, 0) if up else (1, 3)
            pltpu.make_async_remote_copy(
                fld.at[k, src, c], fld.at[k, dst, c], y_send.at[int(up)],
                y_recv.at[k, int(up), c], device_id=target, device_id_type=MESH,
            ).start()

        @pl.when(core == 0)
        def _():
            planes(True, near)

        @pl.when(core == 1)
        def _():
            planes(False, near)

        @pl.when((core == 1) & (x < 3))
        def _():
            planes(True, far)

        @pl.when((core == 0) & (x > 0))
        def _():
            planes(False, far)

        for p in range(2):
            part = pl.ds(16 * p, 16)
            tiles = fld[k, 1 + p, c].reshape(16, 8, 256)
            xsend[k, 0, c, part] = tiles[:, 0]
            xsend[k, 1, c, part] = tiles[:, 7]
        for side, wraps in ((0, myj == 0), (1, myj == 15)):

            @pl.when(wraps)
            def _():
                turned = signed(c, reflect_z(xsend[k, side, c]))
                for p in range(2):
                    xsend[k, side, c, pl.ds(16 * p, 8)] = turned[16 * p + 8 : 16 * p + 16]
                    xsend[k, side, c, pl.ds(16 * p + 8, 8)] = turned[16 * p : 16 * p + 8]

        for side, (cy, cz) in ((0, left), (1, right)):
            pltpu.make_async_remote_copy(
                xsend.at[k, side, c], xrecv.at[k, 1 - side, c], x_send,
                x_recv.at[k, 1 - side, c], device_id=device(x, cy, cz, core), device_id_type=MESH,
            ).start()

    def wait_for(ref, sem):
        pltpu.make_async_copy(ref, ref, sem).wait()

    def wait_halo(k, c):
        for side in range(2):
            wait_for(xrecv.at[k, side, c], x_recv.at[k, side, c])

        @pl.when(jnp.logical_not(bottom))
        def _():
            wait_for(fld.at[k, 0, c], y_recv.at[k, 1, c])

        @pl.when(jnp.logical_not(top))
        def _():
            wait_for(fld.at[k, 3, c], y_recv.at[k, 0, c])

    row = lax.broadcasted_iota(jnp.int32, (32, 256), 0) % 8

    def spread(v):
        return jnp.broadcast_to(v[:, None, :], (4, 8, 256)).reshape(32, 256)

    def speed_of(p):
        plane = (4 * x + 2 * core + p).astype(F32)
        return 2.0 * (plane + 0.5) / 16 - 1.0

    def inner(k, c, p, q, scale):
        part = pl.ds(q * 32, 32)
        v = fld[k, 1 + p, c, part]
        xm = jnp.where(row == 0, 0.0, pltpu.roll(v, 1, 0))
        xp = jnp.where(row == 7, 0.0, pltpu.roll(v, 31, 0))
        total = fld[k, 2 - p, c, part] + xm + xp
        total = total + pltpu.roll(v, 1, 1) + pltpu.roll(v, 255, 1) - 6.0 * v
        return part, scale * total + speed_of(p) * (0.5 * (xp - xm))

    def outer(k, c, p, q, scale):
        part = pl.ds(q * 32, 32)
        edge = pl.ds(pl.multiple_of(16 * p, 16), 16)
        half = 0.5 * speed_of(p)
        before = spread((scale - half) * xrecv[k, 0, c, edge][q * 4 : q * 4 + 4])
        after = spread((scale + half) * xrecv[k, 1, c, edge][q * 4 : q * 4 + 4])
        rows = jnp.where(row == 0, before, jnp.where(row == 7, after, 0.0))
        return part, scale * fld[k, 3 * p, c, part] + rows

    def tiles(body):
        def step(p, carry):
            for q in range(4):
                body(p, q)
            return carry

        lax.fori_loop(0, 2, step, 0)

    def derive(k, c):
        for p in range(2):
            dbuf[c, p] = jnp.dot(
                kmat[...], fld[k, 1 + p, c], preferred_element_type=F32,
                precision=lax.Precision.HIGHEST,
            )

    def symmetrize(c):
        wait_for(rbuf[c], in_recv.at[c])

        def take(p, t, half):
            return rbuf[c][p, inv[t % 16], half]

        for p in range(2):
            other = jnp.concatenate([take(p, t + 8, 1) for t in range(16)], axis=0)
            own = jnp.concatenate([take(p, t, 0) for t in range(16)], axis=0)
            fld[0, 1 + p, c] = 0.5 * (own + signed(c, reflect_z(other)))
        send_halo(0, c)

    def residual_inner(c, omega):
        derive(0, c)

        def body(p, q):
            part, value = inner(0, c, p, q, -VISCOSITY)
            fld[1, 1 + p, c, part] = omega * dbuf[c, p, part] + value

        tiles(body)

    def residual_outer(c):
        wait_halo(0, c)

        def body(p, q):
            part, value = outer(0, c, p, q, -VISCOSITY)
            value = fld[1, 1 + p, c, part] + value
            fld[1, 1 + p, c, part] = value
            acc[0] += value * dbuf[c, p, part]

        tiles(body)

    def prepare_inner(c):
        derive(2, c)

        def body(p, q):
            part, value = inner(2, c, p, q, -VISCOSITY)
            fld[3, 1 + p, c, part] = value

        tiles(body)

    def prepare_outer(c):
        wait_halo(2, c)

        def body(p, q):
            part, value = outer(2, c, p, q, -VISCOSITY)
            fld[3, 1 + p, c, part] += value

        tiles(body)

    def complete(c, omega):
        def body(p, q):
            part = pl.ds(q * 32, 32)
            d = dbuf[c, p, part]
            value = omega * d + fld[3, 1 + p, c, part]
            fld[3, 1 + p, c, part] = value
            acc[1] += value * d

        tiles(body)
        send_halo(3, c)

    def field_inner(k, c, omega):
        derive(k, c)

        def body(p, q):
            part, value = inner(k, c, p, q, VISCOSITY)
            dbuf[c, p, part] = omega * dbuf[c, p, part] + value

        tiles(body)

    def field_outer(k, c, store):
        wait_halo(k, c)

        def body(p, q):
            part, value = outer(k, c, p, q, VISCOSITY)
            rate = dbuf[c, p, part] + value
            store(p, part, fld[k - 1, 1 + p, c, part] + DESCENT * rate)

        tiles(body)

    def next_outer(c):
        def store(p, part, value):
            fld[2, 1 + p, c, part] = value

        field_outer(1, c, store)
        send_halo(2, c)

    stages = (
        (0, 16, y * 4 + z, lambda r: device(x, r // 4, r % 4, core)),
        (16, 8, x * 2 + core, lambda r: device(r // 2, y, z, r % 2)),
    )

    def drift_send(it, stage, tile):
        base, size, rank, of = stages[stage]
        drift[it, base + rank] = tile

        def body(k, carry):
            pltpu.make_async_remote_copy(
                drift.at[it, base + rank], drift.at[it, base + rank], d_send,
                d_recv.at[it, stage], device_id=of((rank + k) % size), device_id_type=MESH,
            ).start()
            return carry

        lax.fori_loop(1, size, body, 0)

    def drift_sum(it, stage):
        base, size, _, _ = stages[stage]
        wait_for(drift.at[it, pl.ds(base, size - 1)], d_recv.at[it, stage])
        tile = drift[it, base]
        for k in range(1, size):
            tile = tile + drift[it, base + k]
        return tile

    def drift_start(it):
        a = acc[it]
        tile = a[0:8] + a[8:16] + a[16:24] + a[24:32]
        drift_send(it, 0, tile[:, :128] + tile[:, 128:])

    entries = 16 * 3 * 16 * 256 * 256

    def drift_end(it, omega):
        return omega - FREQUENCY_RATE * (jnp.sum(drift_sum(it, 1)) / (entries // 2))

    def send_out(o, c, source):
        for p in range(2):
            value = source(p)[...]
            turned = signed(c, reflect_z(value)).reshape(16, 8, 256)
            mbuf[p, 0] = value.reshape(16, 8, 256)
            mbuf[p, 1, 0:8] = turned[8:16]
            mbuf[p, 1, 8:16] = turned[0:8]

            def build(i, carry):
                for s in range(2):
                    t = times[2 * i + s]
                    obuf[o, c, p * 8 + i, s, 0] = mbuf[p, 0, t]
                    obuf[o, c, p * 8 + i, s, 1] = mbuf[p, 1, t]
                return carry

            lax.fori_loop(0, 8, build, 0)

            def body(k, carry):
                di = (inst + k) % 8
                ds = x * 4 + core * 2 + p
                src = obuf.at[o, c, p * 8 + di]
                dst = outs[o].at[:, c, :, myj]
                mine = (di == inst) & (ds == space)

                @pl.when(mine)
                def _():
                    pltpu.make_async_copy(src, dst, o_recv.at[o]).start()

                @pl.when(jnp.logical_not(mine))
                def _():
                    pltpu.make_async_remote_copy(
                        src, dst, o_send.at[o], o_recv.at[o], device_id=(di, ds),
                        device_id_type=MESH,
                    ).start()

                return carry

            lax.fori_loop(0, 8, body, 0)

    acc[...] = jnp.zeros(acc.shape, F32)
    omega = freq[0]
    for c in range(3):
        symmetrize(c)
        residual_inner(c, omega)
    for c in range(3):
        residual_outer(c)
        if c == 2:
            drift_start(0)
        send_halo(1, c)
    for c in range(3):
        field_inner(1, c, omega)
    next_outer(0)
    drift_send(0, 1, drift_sum(0, 0))
    prepare_inner(0)
    next_outer(1)
    next_outer(2)
    prepare_outer(0)
    omega = drift_end(0, omega)
    for c in range(3):
        if c > 0:
            prepare_inner(c)
            prepare_outer(c)
        complete(c, omega)
        if c == 2:
            drift_start(1)
        send_out(0, c, lambda p: fld.at[3, 1 + p, c])
    for c in range(3):
        field_inner(3, c, omega)

        def keep(p, part, value):
            orb[p, part] = value

        field_outer(3, c, keep)
        if c == 0:
            drift_send(1, 1, drift_sum(1, 0))
        send_out(1, c, lambda p: orb.at[p])
    freq[0] = drift_end(1, omega)
    result = pltpu.make_async_copy(freq, fout, small.at[0])
    result.start()
    result.wait()

    for o in range(2):
        wait_for(outs[o], o_recv.at[o])
    part = pl.ds(0, 15)

    @pl.when(core == yhi)
    def _():
        wait_for(vel.at[:, :, :, part], in_send)
        for o in range(2):
            wait_for(obuf.at[o, :, part], o_send.at[o])

    @pl.when(core != yhi)
    def _():
        wait_for(vel, in_send)
        for o in range(2):
            wait_for(obuf.at[o], o_send.at[o])

    wait_for(xsend, x_send)

    @pl.when(jnp.logical_not(top))
    def _():
        wait_for(fld.at[:, 2], y_send.at[1])

    @pl.when(jnp.logical_not(bottom))
    def _():
        wait_for(fld.at[:, 1], y_send.at[0])

    wait_for(drift.at[:, pl.ds(0, 22)], d_send)


def finish(orbit, defect, new, orbit_out, defect_out, new_out, one, sems):
    first = pltpu.make_async_copy(new, one, sems.at[0])
    first.start()
    copies = [
        pltpu.make_async_copy(src.at[s], dst.at[s], sems.at[1 + 2 * k + s])
        for k, (src, dst) in enumerate(((orbit, orbit_out), (defect, defect_out)))
        for s in range(2)
    ]
    for copy in copies:
        copy.start()
    first.wait()
    copies.append(pltpu.make_async_copy(one, new_out, sems.at[5]))
    copies[-1].start()
    for copy in copies:
        copy.wait()


def shards(velocity, frequency, slot_time, mirror_rows):
    cut = (2, 3, 2, 16, 8, 256)
    whole = jax.ShapeDtypeStruct(cut, F32)
    shapes = (whole, whole, jax.ShapeDtypeStruct((1,), F32))
    hbm = pl.BlockSpec(memory_space=pltpu.HBM)
    vmem = pl.BlockSpec(memory_space=pltpu.VMEM)
    dma = pltpu.SemaphoreType.DMA
    results = pl.pallas_call(
        kernel,
        out_shape=(pltpu.VMEM(cut, F32), pltpu.VMEM(cut, F32), shapes[2]),
        in_specs=[hbm] * 4,
        out_specs=(vmem, vmem, hbm),
        scratch_shapes=[
            pltpu.SMEM((1,), F32),
            pltpu.SMEM((16,), jnp.int32),
            pltpu.VMEM((1, 256), jnp.int32),
            pltpu.VMEM((2, 16, 2, 8, 256), F32),
            pltpu.VMEM((2, 16, 2, 8, 256), F32),
            pltpu.VMEM((2, 16, 2, 8, 256), F32),
            pltpu.VMEM((4, 4, 3, 128, 256), F32),
            pltpu.VMEM((2, 128, 256), F32),
            pltpu.VMEM((4, 2, 3, 32, 256), F32),
            pltpu.VMEM((4, 2, 3, 32, 256), F32),
            pltpu.VMEM((2, 3, 16, 2, 2, 8, 256), F32),
            pltpu.VMEM((2, 2, 16, 8, 256), F32),
            pltpu.VMEM((3, 2, 128, 256), F32),
            pltpu.VMEM((256, 256), jnp.bfloat16),
            pltpu.VMEM((128, 128), F32),
            pltpu.VMEM((2, 32, 256), F32),
            pltpu.VMEM((2, 24, 8, 128), F32),
            pltpu.SMEM((16,), jnp.int32),
            dma((3,)),
            dma,
            dma((3,)),
            dma,
            dma((4, 2, 3)),
            dma((2,)),
            dma((4, 2, 3)),
            dma((2,)),
            dma((2,)),
            dma,
            dma((2, 2)),
        ],
        compiler_params=pltpu.CompilerParams(
            collective_id=0, has_side_effects=True, vmem_limit_bytes=40 * 1024 * 1024
        ),
    )(frequency, *[
        pltpu.with_memory_space_constraint(v, pltpu.HBM)
        for v in (slot_time, mirror_rows.reshape(1, 256), velocity.reshape(cut))
    ])
    orbit, defect, new = pl.pallas_call(
        finish,
        out_shape=shapes,
        in_specs=[vmem, vmem, hbm],
        out_specs=(hbm,) * 3,
        scratch_shapes=[pltpu.SMEM((1,), F32), dma((6,))],
        compiler_params=pltpu.CompilerParams(vmem_limit_bytes=4 * 1024 * 1024),
    )(*results)
    return orbit.reshape(velocity.shape), defect.reshape(velocity.shape), new


def solution(mesh):
    spread = P("inst", None, "space", None, None)
    return jax.shard_map(
        shards, mesh=mesh, in_specs=(spread, P(), P(), P()), out_specs=(spread, spread, P()),
        check_vma=False,
    )
```

```python
import functools
import math

import jax
import jax.numpy as jnp
from jax import lax
from jax.experimental import pallas as pl
from jax.experimental.pallas import tpu as pltpu
from jax.sharding import PartitionSpec as P

VISCOSITY = 0.5
DESCENT = 0.001
FREQUENCY_RATE = 0.025
MESH = pl.DeviceIdType.MESH
F32 = jnp.float32


def device(x, y, z, core):
    return ((y % 2) * 4 + z, x * 4 + (y // 2) * 2 + core)


def chip_of(j):
    y = j // 4
    r = j % 4
    return y, jnp.where(y % 2 == 0, r, 3 - r)


def weight(k):
    k = k % 16
    if k == 0:
        return 0.0
    angle = math.pi * k / 16
    return 0.5 * (-1.0) ** k * math.cos(angle) / math.sin(angle)


def kernel(
    freq_in, times_in, mirror_in, vel, orbit, defect, fout, freq, times, mirror,
    rbuf0, rbuf1, rbuf2, fld, orb, xsend, xrecv, obuf, mbuf, dbuf, mat, kmat, acc, drift, inv,
    small, in_send, in_recv, x_send, x_recv, y_send, y_recv, o_send, o_recv, d_send, d_recv,
):
    inst = lax.axis_index("inst")
    space = lax.axis_index("space")
    z = inst % 4
    yhi = space // 2 % 2
    y = yhi * 2 + inst // 4
    x = space // 4
    core = space % 2
    myj = y * 4 + jnp.where(y % 2 == 0, z, 3 - z)
    outs = (defect, orbit)
    rbuf = (rbuf0, rbuf1, rbuf2)

    barrier = pltpu.get_barrier_semaphore()

    steps = sorted(
        ((dy, dz, dc) for dy in range(4) for dz in range(4) for dc in range(2)),
        key=lambda d: -min(d[0], 4 - d[0]) - min(d[1], 4 - d[1]),
    )
    friends = [
        device(x, (y + dy) % 4, (z + dz) % 4, (core + dc) % 2)
        for dy, dz, dc in steps if dy + dz > 0
    ]
    friends += [device((x + 1 + k // 2) % 4, y, z, (core + k) % 2) for k in (2, 3, 0, 1, 4, 5)]
    friends += [device(x, y, z, 1 - core)]
    for friend in friends:
        pl.semaphore_signal(barrier, inc=1, device_id=friend, device_id_type=MESH)
    far = device((x + jnp.where(core == 1, 1, 3)) % 4, y, z, 1 - core)
    near = device(x, y, z, 1 - core)
    fetches = [
        pltpu.make_async_copy(src, dst, small.at[k])
        for k, (src, dst) in enumerate(
            ((freq_in, freq), (times_in, times), (mirror_in, mirror))
        )
    ]
    for copy in fetches:
        copy.start()
    pl.semaphore_wait(barrier, len(friends))

    def send_in(c):
        def body(k, carry):
            j = (k + myj) % 16
            cy, cz = chip_of(j)
            di, ds = device(x, cy, cz, yhi)
            src = vel.at[:, c, :, j]
            dst = rbuf[c].at[core, pl.ds(2 * inst, 2)]
            mine = (di == inst) & (ds == space)

            @pl.when(mine)
            def _():
                pltpu.make_async_copy(src, dst, in_recv.at[c]).start()

            @pl.when(jnp.logical_not(mine))
            def _():
                pltpu.make_async_remote_copy(
                    src, dst, in_send, in_recv.at[c], device_id=(di, ds), device_id_type=MESH
                ).start()

            return carry

        lax.fori_loop(0, 16, body, 0)

    for c in range(3):
        send_in(c)

    for copy in fetches:
        copy.wait()
    mat[...] = (
        lax.broadcasted_iota(jnp.int32, (256, 256), 0) == mirror[...]
    ).astype(F32).astype(jnp.bfloat16)
    rows = lax.broadcasted_iota(jnp.int32, (128, 128), 0)
    cols = lax.broadcasted_iota(jnp.int32, (128, 128), 1)
    gap = (rows // 8 - cols // 8 + 16) % 16
    table = jnp.zeros((128, 128), F32)
    for k in range(1, 16):
        table = jnp.where(gap == k, jnp.float32(weight(k)), table)
    kmat[...] = jnp.where(rows % 8 == cols % 8, table, 0.0)

    def invert(t, carry):
        def find(s, found):
            return jnp.where(times[s] == t, s, found)

        inv[t] = lax.fori_loop(0, 16, find, jnp.int32(0))
        return carry

    lax.fori_loop(0, 16, invert, 0)
    bottom = (x == 0) & (core == 0)
    top = (x == 3) & (core == 1)

    @pl.when(bottom)
    def _():
        fld[:, 0] = jnp.zeros((4, 3, 128, 256), F32)

    @pl.when(top)
    def _():
        fld[:, 3] = jnp.zeros((4, 3, 128, 256), F32)

    def reflect_z(v):
        high = v.astype(jnp.bfloat16)
        rest = v - high.astype(F32)
        middle = rest.astype(jnp.bfloat16)
        low = (rest - middle.astype(F32)).astype(jnp.bfloat16)
        m = mat[...]
        parts = [jnp.dot(u, m, preferred_element_type=F32) for u in (high, middle, low)]
        return parts[0] + (parts[1] + parts[2])

    def signed(c, v):
        return -v if c == 2 else v

    left = chip_of((myj + 15) % 16)
    right = chip_of((myj + 1) % 16)

    def send_halo(k, c):
        def planes(up, target):
            src, dst = (2, 0) if up else (1, 3)
            pltpu.make_async_remote_copy(
                fld.at[k, src, c], fld.at[k, dst, c], y_send.at[int(up)],
                y_recv.at[k, int(up), c], device_id=target, device_id_type=MESH,
            ).start()

        @pl.when(core == 0)
        def _():
            planes(True, near)

        @pl.when(core == 1)
        def _():
            planes(False, near)

        @pl.when((core == 1) & (x < 3))
        def _():
            planes(True, far)

        @pl.when((core == 0) & (x > 0))
        def _():
            planes(False, far)

        for p in range(2):
            part = pl.ds(16 * p, 16)
            tiles = fld[k, 1 + p, c].reshape(16, 8, 256)
            xsend[k, 0, c, part] = tiles[:, 0]
            xsend[k, 1, c, part] = tiles[:, 7]
        for side, wraps in ((0, myj == 0), (1, myj == 15)):

            @pl.when(wraps)
            def _():
                turned = signed(c, reflect_z(xsend[k, side, c]))
                for p in range(2):
                    xsend[k, side, c, pl.ds(16 * p, 8)] = turned[16 * p + 8 : 16 * p + 16]
                    xsend[k, side, c, pl.ds(16 * p + 8, 8)] = turned[16 * p : 16 * p + 8]

        for side, (cy, cz) in ((0, left), (1, right)):
            pltpu.make_async_remote_copy(
                xsend.at[k, side, c], xrecv.at[k, 1 - side, c], x_send,
                x_recv.at[k, 1 - side, c], device_id=device(x, cy, cz, core), device_id_type=MESH,
            ).start()

    def wait_for(ref, sem):
        pltpu.make_async_copy(ref, ref, sem).wait()

    def wait_halo(k, c):
        for side in range(2):
            wait_for(xrecv.at[k, side, c], x_recv.at[k, side, c])

        @pl.when(jnp.logical_not(bottom))
        def _():
            wait_for(fld.at[k, 0, c], y_recv.at[k, 1, c])

        @pl.when(jnp.logical_not(top))
        def _():
            wait_for(fld.at[k, 3, c], y_recv.at[k, 0, c])

    row = lax.broadcasted_iota(jnp.int32, (32, 256), 0) % 8

    def spread(v):
        return jnp.broadcast_to(v[:, None, :], (4, 8, 256)).reshape(32, 256)

    def speed_of(p):
        plane = (4 * x + 2 * core + p).astype(F32)
        return 2.0 * (plane + 0.5) / 16 - 1.0

    def inner(k, c, p, q, scale):
        part = pl.ds(q * 32, 32)
        v = fld[k, 1 + p, c, part]
        xm = jnp.where(row == 0, 0.0, pltpu.roll(v, 1, 0))
        xp = jnp.where(row == 7, 0.0, pltpu.roll(v, 31, 0))
        total = fld[k, 2 - p, c, part] + xm + xp
        total = total + pltpu.roll(v, 1, 1) + pltpu.roll(v, 255, 1) - 6.0 * v
        return part, scale * total + speed_of(p) * (0.5 * (xp - xm))

    def outer(k, c, p, q, scale):
        part = pl.ds(q * 32, 32)
        edge = pl.ds(pl.multiple_of(16 * p, 16), 16)
        half = 0.5 * speed_of(p)
        before = spread((scale - half) * xrecv[k, 0, c, edge][q * 4 : q * 4 + 4])
        after = spread((scale + half) * xrecv[k, 1, c, edge][q * 4 : q * 4 + 4])
        rows = jnp.where(row == 0, before, jnp.where(row == 7, after, 0.0))
        return part, scale * fld[k, 3 * p, c, part] + rows

    def tiles(body):
        def step(p, carry):
            for q in range(4):
                body(p, q)
            return carry

        lax.fori_loop(0, 2, step, 0)

    def derive(k, c):
        for p in range(2):
            dbuf[c, p] = jnp.dot(
                kmat[...], fld[k, 1 + p, c], preferred_element_type=F32,
                precision=lax.Precision.HIGHEST,
            )

    def symmetrize(c):
        wait_for(rbuf[c], in_recv.at[c])

        def take(p, t, half):
            return rbuf[c][p, inv[t % 16], half]

        for p in range(2):
            other = jnp.concatenate([take(p, t + 8, 1) for t in range(16)], axis=0)
            own = jnp.concatenate([take(p, t, 0) for t in range(16)], axis=0)
            fld[0, 1 + p, c] = 0.5 * (own + signed(c, reflect_z(other)))
        send_halo(0, c)

    def residual_inner(c, omega):
        derive(0, c)

        def body(p, q):
            part, value = inner(0, c, p, q, -VISCOSITY)
            fld[1, 1 + p, c, part] = omega * dbuf[c, p, part] + value

        tiles(body)

    def residual_outer(c):
        wait_halo(0, c)

        def body(p, q):
            part, value = outer(0, c, p, q, -VISCOSITY)
            value = fld[1, 1 + p, c, part] + value
            fld[1, 1 + p, c, part] = value
            acc[0] += value * dbuf[c, p, part]

        tiles(body)

    def prepare_inner(c):
        derive(2, c)

        def body(p, q):
            part, value = inner(2, c, p, q, -VISCOSITY)
            fld[3, 1 + p, c, part] = value

        tiles(body)

    def prepare_outer(c):
        wait_halo(2, c)

        def body(p, q):
            part, value = outer(2, c, p, q, -VISCOSITY)
            fld[3, 1 + p, c, part] += value

        tiles(body)

    def complete(c, omega):
        def body(p, q):
            part = pl.ds(q * 32, 32)
            d = dbuf[c, p, part]
            value = omega * d + fld[3, 1 + p, c, part]
            fld[3, 1 + p, c, part] = value
            acc[1] += value * d

        tiles(body)
        send_halo(3, c)

    def field_inner(k, c, omega):
        derive(k, c)

        def body(p, q):
            part, value = inner(k, c, p, q, VISCOSITY)
            dbuf[c, p, part] = omega * dbuf[c, p, part] + value

        tiles(body)

    def field_outer(k, c, store):
        wait_halo(k, c)

        def body(p, q):
            part, value = outer(k, c, p, q, VISCOSITY)
            rate = dbuf[c, p, part] + value
            store(p, part, fld[k - 1, 1 + p, c, part] + DESCENT * rate)

        tiles(body)

    def next_outer(c):
        def store(p, part, value):
            fld[2, 1 + p, c, part] = value

        field_outer(1, c, store)
        send_halo(2, c)

    stages = (
        (0, 16, y * 4 + z, lambda r: device(x, r // 4, r % 4, core)),
        (16, 8, x * 2 + core, lambda r: device(r // 2, y, z, r % 2)),
    )

    def drift_send(it, stage, tile):
        base, size, rank, of = stages[stage]
        drift[it, base + rank] = tile

        def body(k, carry):
            pltpu.make_async_remote_copy(
                drift.at[it, base + rank], drift.at[it, base + rank], d_send,
                d_recv.at[it, stage], device_id=of((rank + k) % size), device_id_type=MESH,
            ).start()
            return carry

        lax.fori_loop(1, size, body, 0)

    def drift_sum(it, stage):
        base, size, _, _ = stages[stage]
        wait_for(drift.at[it, pl.ds(base, size - 1)], d_recv.at[it, stage])
        tile = drift[it, base]
        for k in range(1, size):
            tile = tile + drift[it, base + k]
        return tile

    def drift_start(it):
        a = acc[it]
        tile = a[0:8] + a[8:16] + a[16:24] + a[24:32]
        drift_send(it, 0, tile[:, :128] + tile[:, 128:])

    entries = 16 * 3 * 16 * 256 * 256

    def drift_end(it, omega):
        return omega - FREQUENCY_RATE * (jnp.sum(drift_sum(it, 1)) / (entries // 2))

    def send_out(o, c, source):
        for p in range(2):
            value = source(p)[...]
            turned = signed(c, reflect_z(value)).reshape(16, 8, 256)
            mbuf[p, 0] = value.reshape(16, 8, 256)
            mbuf[p, 1, 0:8] = turned[8:16]
            mbuf[p, 1, 8:16] = turned[0:8]

            def build(i, carry):
                for s in range(2):
                    t = times[2 * i + s]
                    obuf[o, c, p * 8 + i, s, 0] = mbuf[p, 0, t]
                    obuf[o, c, p * 8 + i, s, 1] = mbuf[p, 1, t]
                return carry

            lax.fori_loop(0, 8, build, 0)

            def body(k, carry):
                di = (inst + 1 + k) % 8
                ds = x * 4 + core * 2 + p
                src = obuf.at[o, c, p * 8 + di]
                dst = outs[o].at[:, c, :, myj]
                mine = (di == inst) & (ds == space)

                @pl.when(mine)
                def _():
                    pltpu.make_async_copy(src, dst, o_recv.at[o]).start()

                @pl.when(jnp.logical_not(mine))
                def _():
                    pltpu.make_async_remote_copy(
                        src, dst, o_send.at[o], o_recv.at[o], device_id=(di, ds),
                        device_id_type=MESH,
                    ).start()

                return carry

            lax.fori_loop(0, 8, body, 0)

    acc[...] = jnp.zeros(acc.shape, F32)
    omega = freq[0]
    for c in range(3):
        symmetrize(c)
        residual_inner(c, omega)
    for c in range(3):
        residual_outer(c)
        if c == 2:
            drift_start(0)
        send_halo(1, c)
    for c in range(3):
        field_inner(1, c, omega)
    next_outer(0)
    drift_send(0, 1, drift_sum(0, 0))
    prepare_inner(0)
    next_outer(1)
    next_outer(2)
    prepare_outer(0)
    prepare_inner(1)
    prepare_inner(2)
    omega = drift_end(0, omega)
    for c in range(3):
        if c > 0:
            prepare_outer(c)
        complete(c, omega)
    drift_start(1)
    for c in range(3):
        send_out(0, c, lambda p: fld.at[3, 1 + p, c])
    for c in range(3):
        field_inner(3, c, omega)

        def keep(p, part, value):
            orb[p, part] = value

        field_outer(3, c, keep)
        send_out(1, c, lambda p: orb.at[p])
    drift_send(1, 1, drift_sum(1, 0))
    freq[0] = drift_end(1, omega)
    result = pltpu.make_async_copy(freq, fout, small.at[0])
    result.start()
    result.wait()

    for o in range(2):
        wait_for(outs[o], o_recv.at[o])
    part = pl.ds(0, 15)

    @pl.when(core == yhi)
    def _():
        wait_for(vel.at[:, :, :, part], in_send)
        for o in range(2):
            wait_for(obuf.at[o, :, part], o_send.at[o])

    @pl.when(core != yhi)
    def _():
        wait_for(vel, in_send)
        for o in range(2):
            wait_for(obuf.at[o], o_send.at[o])

    wait_for(xsend, x_send)

    @pl.when(jnp.logical_not(top))
    def _():
        wait_for(fld.at[:, 2], y_send.at[1])

    @pl.when(jnp.logical_not(bottom))
    def _():
        wait_for(fld.at[:, 1], y_send.at[0])

    wait_for(drift.at[:, pl.ds(0, 22)], d_send)


def finish(orbit, defect, new, orbit_out, defect_out, new_out, one, sems):
    first = pltpu.make_async_copy(new, one, sems.at[0])
    first.start()
    copies = [
        pltpu.make_async_copy(src.at[s], dst.at[s], sems.at[1 + 2 * k + s])
        for k, (src, dst) in enumerate(((orbit, orbit_out), (defect, defect_out)))
        for s in range(2)
    ]
    for copy in copies:
        copy.start()
    first.wait()
    copies.append(pltpu.make_async_copy(one, new_out, sems.at[5]))
    copies[-1].start()
    for copy in copies:
        copy.wait()


def shards(velocity, frequency, slot_time, mirror_rows):
    cut = (2, 3, 2, 16, 8, 256)
    whole = jax.ShapeDtypeStruct(cut, F32)
    shapes = (whole, whole, jax.ShapeDtypeStruct((1,), F32))
    hbm = pl.BlockSpec(memory_space=pltpu.HBM)
    vmem = pl.BlockSpec(memory_space=pltpu.VMEM)
    dma = pltpu.SemaphoreType.DMA
    results = pl.pallas_call(
        kernel,
        out_shape=(pltpu.VMEM(cut, F32), pltpu.VMEM(cut, F32), shapes[2]),
        in_specs=[hbm] * 4,
        out_specs=(vmem, vmem, hbm),
        scratch_shapes=[
            pltpu.SMEM((1,), F32),
            pltpu.SMEM((16,), jnp.int32),
            pltpu.VMEM((1, 256), jnp.int32),
            pltpu.VMEM((2, 16, 2, 8, 256), F32),
            pltpu.VMEM((2, 16, 2, 8, 256), F32),
            pltpu.VMEM((2, 16, 2, 8, 256), F32),
            pltpu.VMEM((4, 4, 3, 128, 256), F32),
            pltpu.VMEM((2, 128, 256), F32),
            pltpu.VMEM((4, 2, 3, 32, 256), F32),
            pltpu.VMEM((4, 2, 3, 32, 256), F32),
            pltpu.VMEM((2, 3, 16, 2, 2, 8, 256), F32),
            pltpu.VMEM((2, 2, 16, 8, 256), F32),
            pltpu.VMEM((3, 2, 128, 256), F32),
            pltpu.VMEM((256, 256), jnp.bfloat16),
            pltpu.VMEM((128, 128), F32),
            pltpu.VMEM((2, 32, 256), F32),
            pltpu.VMEM((2, 24, 8, 128), F32),
            pltpu.SMEM((16,), jnp.int32),
            dma((3,)),
            dma,
            dma((3,)),
            dma,
            dma((4, 2, 3)),
            dma((2,)),
            dma((4, 2, 3)),
            dma((2,)),
            dma((2,)),
            dma,
            dma((2, 2)),
        ],
        compiler_params=pltpu.CompilerParams(
            collective_id=0, has_side_effects=True, vmem_limit_bytes=40 * 1024 * 1024
        ),
    )(frequency, *[
        pltpu.with_memory_space_constraint(v, pltpu.HBM)
        for v in (slot_time, mirror_rows.reshape(1, 256), velocity.reshape(cut))
    ])
    orbit, defect, new = pl.pallas_call(
        finish,
        out_shape=shapes,
        in_specs=[vmem, vmem, hbm],
        out_specs=(hbm,) * 3,
        scratch_shapes=[pltpu.SMEM((1,), F32), dma((6,))],
        compiler_params=pltpu.CompilerParams(vmem_limit_bytes=4 * 1024 * 1024),
    )(*results)
    return orbit.reshape(velocity.shape), defect.reshape(velocity.shape), new


def solution(mesh):
    spread = P("inst", None, "space", None, None)
    return jax.shard_map(
        shards, mesh=mesh, in_specs=(spread, P(), P(), P()), out_specs=(spread, spread, P()),
        check_vma=False,
    )
```

```python
import functools
import math

import jax
import jax.numpy as jnp
from jax import lax
from jax.experimental import pallas as pl
from jax.experimental.pallas import tpu as pltpu
from jax.sharding import PartitionSpec as P

VISCOSITY = 0.5
DESCENT = 0.001
FREQUENCY_RATE = 0.025
MESH = pl.DeviceIdType.MESH
F32 = jnp.float32


def device(x, y, z, core):
    return ((y % 2) * 4 + z, x * 4 + (y // 2) * 2 + core)


def chip_of(j):
    y = j // 4
    r = j % 4
    return y, jnp.where(y % 2 == 0, r, 3 - r)


def weight(k):
    k = k % 16
    if k == 0:
        return 0.0
    angle = math.pi * k / 16
    return 0.5 * (-1.0) ** k * math.cos(angle) / math.sin(angle)


def kernel(
    freq_in, times_in, mirror_in, vel, orbit, defect, fout, freq, times, mirror,
    rbuf0, rbuf1, rbuf2, fld, orb, xsend, xrecv, obuf, mbuf, dbuf, mat, kmat, acc, drift, inv,
    small, in_send, in_recv, x_send, x_recv, y_send, y_recv, o_send, o_recv, d_send, d_recv,
):
    inst = lax.axis_index("inst")
    space = lax.axis_index("space")
    z = inst % 4
    yhi = space // 2 % 2
    y = yhi * 2 + inst // 4
    x = space // 4
    core = space % 2
    myj = y * 4 + jnp.where(y % 2 == 0, z, 3 - z)
    outs = (defect, orbit)
    rbuf = (rbuf0, rbuf1, rbuf2)

    barrier = pltpu.get_barrier_semaphore()

    steps = sorted(
        ((dy, dz, dc) for dy in range(4) for dz in range(4) for dc in range(2)),
        key=lambda d: -min(d[0], 4 - d[0]) - min(d[1], 4 - d[1]),
    )
    friends = [
        device(x, (y + dy) % 4, (z + dz) % 4, (core + dc) % 2)
        for dy, dz, dc in steps if dy + dz > 0
    ]
    friends += [device((x + 1 + k // 2) % 4, y, z, (core + k) % 2) for k in (2, 3, 0, 1, 4, 5)]
    friends += [device(x, y, z, 1 - core)]
    for friend in friends:
        pl.semaphore_signal(barrier, inc=1, device_id=friend, device_id_type=MESH)
    far = device((x + jnp.where(core == 1, 1, 3)) % 4, y, z, 1 - core)
    near = device(x, y, z, 1 - core)
    fetches = [
        pltpu.make_async_copy(src, dst, small.at[k])
        for k, (src, dst) in enumerate(
            ((freq_in, freq), (times_in, times), (mirror_in, mirror))
        )
    ]
    for copy in fetches:
        copy.start()
    pl.semaphore_wait(barrier, len(friends))

    def send_in(c):
        def body(k, carry):
            j = (k + myj) % 16
            cy, cz = chip_of(j)
            di, ds = device(x, cy, cz, yhi)
            src = vel.at[:, c, :, j]
            dst = rbuf[c].at[core, pl.ds(2 * inst, 2)]
            mine = (di == inst) & (ds == space)

            @pl.when(mine)
            def _():
                pltpu.make_async_copy(src, dst, in_recv.at[c]).start()

            @pl.when(jnp.logical_not(mine))
            def _():
                pltpu.make_async_remote_copy(
                    src, dst, in_send, in_recv.at[c], device_id=(di, ds), device_id_type=MESH
                ).start()

            return carry

        lax.fori_loop(0, 16, body, 0)

    for c in range(3):
        send_in(c)

    for copy in fetches:
        copy.wait()
    mat[...] = (
        lax.broadcasted_iota(jnp.int32, (256, 256), 0) == mirror[...]
    ).astype(F32).astype(jnp.bfloat16)
    rows = lax.broadcasted_iota(jnp.int32, (128, 128), 0)
    cols = lax.broadcasted_iota(jnp.int32, (128, 128), 1)
    gap = (rows // 8 - cols // 8 + 16) % 16
    table = jnp.zeros((128, 128), F32)
    for k in range(1, 16):
        table = jnp.where(gap == k, jnp.float32(weight(k)), table)
    kmat[...] = jnp.where(rows % 8 == cols % 8, table, 0.0)

    def invert(t, carry):
        def find(s, found):
            return jnp.where(times[s] == t, s, found)

        inv[t] = lax.fori_loop(0, 16, find, jnp.int32(0))
        return carry

    lax.fori_loop(0, 16, invert, 0)
    bottom = (x == 0) & (core == 0)
    top = (x == 3) & (core == 1)

    @pl.when(bottom)
    def _():
        fld[:, 0] = jnp.zeros((4, 3, 128, 256), F32)

    @pl.when(top)
    def _():
        fld[:, 3] = jnp.zeros((4, 3, 128, 256), F32)

    def reflect_z(v):
        high = v.astype(jnp.bfloat16)
        rest = v - high.astype(F32)
        middle = rest.astype(jnp.bfloat16)
        low = (rest - middle.astype(F32)).astype(jnp.bfloat16)
        m = mat[...]
        parts = [jnp.dot(u, m, preferred_element_type=F32) for u in (high, middle, low)]
        return parts[0] + (parts[1] + parts[2])

    def signed(c, v):
        return -v if c == 2 else v

    left = chip_of((myj + 15) % 16)
    right = chip_of((myj + 1) % 16)

    def send_halo(k, c):
        def planes(up, target):
            src, dst = (2, 0) if up else (1, 3)
            pltpu.make_async_remote_copy(
                fld.at[k, src, c], fld.at[k, dst, c], y_send.at[int(up)],
                y_recv.at[k, int(up), c], device_id=target, device_id_type=MESH,
            ).start()

        @pl.when(core == 0)
        def _():
            planes(True, near)

        @pl.when(core == 1)
        def _():
            planes(False, near)

        @pl.when((core == 1) & (x < 3))
        def _():
            planes(True, far)

        @pl.when((core == 0) & (x > 0))
        def _():
            planes(False, far)

        for p in range(2):
            part = pl.ds(16 * p, 16)
            tiles = fld[k, 1 + p, c].reshape(16, 8, 256)
            xsend[k, 0, c, part] = tiles[:, 0]
            xsend[k, 1, c, part] = tiles[:, 7]
        for side, wraps in ((0, myj == 0), (1, myj == 15)):

            @pl.when(wraps)
            def _():
                turned = signed(c, reflect_z(xsend[k, side, c]))
                for p in range(2):
                    xsend[k, side, c, pl.ds(16 * p, 8)] = turned[16 * p + 8 : 16 * p + 16]
                    xsend[k, side, c, pl.ds(16 * p + 8, 8)] = turned[16 * p : 16 * p + 8]

        for side, (cy, cz) in ((0, left), (1, right)):
            pltpu.make_async_remote_copy(
                xsend.at[k, side, c], xrecv.at[k, 1 - side, c], x_send,
                x_recv.at[k, 1 - side, c], device_id=device(x, cy, cz, core), device_id_type=MESH,
            ).start()

    def wait_for(ref, sem):
        pltpu.make_async_copy(ref, ref, sem).wait()

    def wait_halo(k, c):
        for side in range(2):
            wait_for(xrecv.at[k, side, c], x_recv.at[k, side, c])

        @pl.when(jnp.logical_not(bottom))
        def _():
            wait_for(fld.at[k, 0, c], y_recv.at[k, 1, c])

        @pl.when(jnp.logical_not(top))
        def _():
            wait_for(fld.at[k, 3, c], y_recv.at[k, 0, c])

    row = lax.broadcasted_iota(jnp.int32, (32, 256), 0) % 8

    def spread(v):
        return jnp.broadcast_to(v[:, None, :], (4, 8, 256)).reshape(32, 256)

    def speed_of(p):
        plane = (4 * x + 2 * core + p).astype(F32)
        return 2.0 * (plane + 0.5) / 16 - 1.0

    def inner(k, c, p, q, scale):
        part = pl.ds(q * 32, 32)
        v = fld[k, 1 + p, c, part]
        xm = jnp.where(row == 0, 0.0, pltpu.roll(v, 1, 0))
        xp = jnp.where(row == 7, 0.0, pltpu.roll(v, 31, 0))
        total = fld[k, 2 - p, c, part] + xm + xp
        total = total + pltpu.roll(v, 1, 1) + pltpu.roll(v, 255, 1) - 6.0 * v
        return part, scale * total + speed_of(p) * (0.5 * (xp - xm))

    def outer(k, c, p, q, scale):
        part = pl.ds(q * 32, 32)
        edge = pl.ds(pl.multiple_of(16 * p, 16), 16)
        half = 0.5 * speed_of(p)
        before = spread((scale - half) * xrecv[k, 0, c, edge][q * 4 : q * 4 + 4])
        after = spread((scale + half) * xrecv[k, 1, c, edge][q * 4 : q * 4 + 4])
        rows = jnp.where(row == 0, before, jnp.where(row == 7, after, 0.0))
        return part, scale * fld[k, 3 * p, c, part] + rows

    def tiles(body):
        def step(p, carry):
            for q in range(4):
                body(p, q)
            return carry

        lax.fori_loop(0, 2, step, 0)

    def derive(k, c):
        for p in range(2):
            dbuf[c, p] = jnp.dot(
                kmat[...], fld[k, 1 + p, c], preferred_element_type=F32,
                precision=lax.Precision.HIGHEST,
            )

    def symmetrize(c):
        wait_for(rbuf[c], in_recv.at[c])

        def take(p, t, half):
            return rbuf[c][p, inv[t % 16], half]

        for p in range(2):
            other = jnp.concatenate([take(p, t + 8, 1) for t in range(16)], axis=0)
            own = jnp.concatenate([take(p, t, 0) for t in range(16)], axis=0)
            fld[0, 1 + p, c] = 0.5 * (own + signed(c, reflect_z(other)))
        send_halo(0, c)

    def residual_inner(c, omega):
        derive(0, c)

        def body(p, q):
            part, value = inner(0, c, p, q, -VISCOSITY)
            fld[1, 1 + p, c, part] = omega * dbuf[c, p, part] + value

        tiles(body)

    def residual_outer(c):
        wait_halo(0, c)

        def body(p, q):
            part, value = outer(0, c, p, q, -VISCOSITY)
            value = fld[1, 1 + p, c, part] + value
            fld[1, 1 + p, c, part] = value
            acc[0] += value * dbuf[c, p, part]

        tiles(body)

    def prepare_inner(c):
        derive(2, c)

        def body(p, q):
            part, value = inner(2, c, p, q, -VISCOSITY)
            fld[3, 1 + p, c, part] = value

        tiles(body)

    def prepare_outer(c):
        wait_halo(2, c)

        def body(p, q):
            part, value = outer(2, c, p, q, -VISCOSITY)
            fld[3, 1 + p, c, part] += value

        tiles(body)

    def complete(c, omega):
        def body(p, q):
            part = pl.ds(q * 32, 32)
            d = dbuf[c, p, part]
            value = omega * d + fld[3, 1 + p, c, part]
            fld[3, 1 + p, c, part] = value
            acc[1] += value * d

        tiles(body)
        send_halo(3, c)

    def field_inner(k, c, omega):
        derive(k, c)

        def body(p, q):
            part, value = inner(k, c, p, q, VISCOSITY)
            dbuf[c, p, part] = omega * dbuf[c, p, part] + value

        tiles(body)

    def field_outer(k, c, store):
        wait_halo(k, c)

        def body(p, q):
            part, value = outer(k, c, p, q, VISCOSITY)
            rate = dbuf[c, p, part] + value
            store(p, part, fld[k - 1, 1 + p, c, part] + DESCENT * rate)

        tiles(body)

    def next_outer(c):
        def store(p, part, value):
            fld[2, 1 + p, c, part] = value

        field_outer(1, c, store)
        send_halo(2, c)

    def apart(*steps):
        return -sum(min(d, 4 - d) for d in steps)

    turns = [(a, b) for a in range(4) for b in range(4)][1:]
    turns.sort(key=lambda d: apart(*d))
    hops = [(a, b) for a in range(4) for b in range(2)][1:]
    hops.sort(key=lambda d: apart(*d))
    stages = (
        (0, 16, y * 4 + z, [device(x, (y + a) % 4, (z + b) % 4, core) for a, b in turns]),
        (16, 8, x * 2 + core, [device((x + a) % 4, y, z, (core + b) % 2) for a, b in hops]),
    )

    def drift_send(it, stage, tile):
        base, _, rank, partners = stages[stage]
        drift[it, base + rank] = tile
        for partner in partners:
            pltpu.make_async_remote_copy(
                drift.at[it, base + rank], drift.at[it, base + rank], d_send,
                d_recv.at[it, stage], device_id=partner, device_id_type=MESH,
            ).start()

    def drift_sum(it, stage):
        base, size, _, _ = stages[stage]
        wait_for(drift.at[it, pl.ds(base, size - 1)], d_recv.at[it, stage])
        tile = drift[it, base]
        for k in range(1, size):
            tile = tile + drift[it, base + k]
        return tile

    def drift_start(it):
        a = acc[it]
        tile = a[0:8] + a[8:16] + a[16:24] + a[24:32]
        drift_send(it, 0, tile[:, :128] + tile[:, 128:])

    entries = 16 * 3 * 16 * 256 * 256

    def drift_end(it, omega):
        return omega - FREQUENCY_RATE * (jnp.sum(drift_sum(it, 1)) / (entries // 2))

    def send_out(o, c, source):
        for p in range(2):
            value = source(p)[...]
            turned = signed(c, reflect_z(value)).reshape(16, 8, 256)
            mbuf[p, 0] = value.reshape(16, 8, 256)
            mbuf[p, 1, 0:8] = turned[8:16]
            mbuf[p, 1, 8:16] = turned[0:8]

            def build(i, carry):
                for s in range(2):
                    t = times[2 * i + s]
                    obuf[o, c, p * 8 + i, s, 0] = mbuf[p, 0, t]
                    obuf[o, c, p * 8 + i, s, 1] = mbuf[p, 1, t]
                return carry

            lax.fori_loop(0, 8, build, 0)

            def body(k, carry):
                di = (inst + 1 + k) % 8
                ds = x * 4 + core * 2 + p
                src = obuf.at[o, c, p * 8 + di]
                dst = outs[o].at[:, c, :, myj]
                mine = (di == inst) & (ds == space)

                @pl.when(mine)
                def _():
                    pltpu.make_async_copy(src, dst, o_recv.at[o]).start()

                @pl.when(jnp.logical_not(mine))
                def _():
                    pltpu.make_async_remote_copy(
                        src, dst, o_send.at[o], o_recv.at[o], device_id=(di, ds),
                        device_id_type=MESH,
                    ).start()

                return carry

            lax.fori_loop(0, 8, body, 0)

    acc[...] = jnp.zeros(acc.shape, F32)
    omega = freq[0]
    for c in range(3):
        symmetrize(c)
        residual_inner(c, omega)
    for c in range(3):
        residual_outer(c)
        if c == 2:
            drift_start(0)
        send_halo(1, c)
    for c in range(3):
        field_inner(1, c, omega)
    next_outer(0)
    drift_send(0, 1, drift_sum(0, 0))
    prepare_inner(0)
    next_outer(1)
    next_outer(2)
    prepare_outer(0)
    prepare_inner(1)
    prepare_inner(2)
    omega = drift_end(0, omega)
    for c in range(3):
        if c > 0:
            prepare_outer(c)
        complete(c, omega)
    drift_start(1)
    for c in range(3):
        send_out(0, c, lambda p: fld.at[3, 1 + p, c])
    for c in range(3):
        field_inner(3, c, omega)

        def keep(p, part, value):
            orb[p, part] = value

        field_outer(3, c, keep)
        send_out(1, c, lambda p: orb.at[p])
    drift_send(1, 1, drift_sum(1, 0))
    freq[0] = drift_end(1, omega)
    result = pltpu.make_async_copy(freq, fout, small.at[0])
    result.start()
    result.wait()

    for o in range(2):
        wait_for(outs[o], o_recv.at[o])
    part = pl.ds(0, 15)

    @pl.when(core == yhi)
    def _():
        wait_for(vel.at[:, :, :, part], in_send)
        for o in range(2):
            wait_for(obuf.at[o, :, part], o_send.at[o])

    @pl.when(core != yhi)
    def _():
        wait_for(vel, in_send)
        for o in range(2):
            wait_for(obuf.at[o], o_send.at[o])

    wait_for(xsend, x_send)

    @pl.when(jnp.logical_not(top))
    def _():
        wait_for(fld.at[:, 2], y_send.at[1])

    @pl.when(jnp.logical_not(bottom))
    def _():
        wait_for(fld.at[:, 1], y_send.at[0])

    wait_for(drift.at[:, pl.ds(0, 22)], d_send)


def finish(orbit, defect, new, orbit_out, defect_out, new_out, one, sems):
    first = pltpu.make_async_copy(new, one, sems.at[0])
    first.start()
    copies = [
        pltpu.make_async_copy(src.at[s], dst.at[s], sems.at[1 + 2 * k + s])
        for k, (src, dst) in enumerate(((orbit, orbit_out), (defect, defect_out)))
        for s in range(2)
    ]
    for copy in copies:
        copy.start()
    first.wait()
    copies.append(pltpu.make_async_copy(one, new_out, sems.at[5]))
    copies[-1].start()
    for copy in copies:
        copy.wait()


def shards(velocity, frequency, slot_time, mirror_rows):
    cut = (2, 3, 2, 16, 8, 256)
    whole = jax.ShapeDtypeStruct(cut, F32)
    shapes = (whole, whole, jax.ShapeDtypeStruct((1,), F32))
    hbm = pl.BlockSpec(memory_space=pltpu.HBM)
    vmem = pl.BlockSpec(memory_space=pltpu.VMEM)
    dma = pltpu.SemaphoreType.DMA
    results = pl.pallas_call(
        kernel,
        out_shape=(pltpu.VMEM(cut, F32), pltpu.VMEM(cut, F32), shapes[2]),
        in_specs=[hbm] * 4,
        out_specs=(vmem, vmem, hbm),
        scratch_shapes=[
            pltpu.SMEM((1,), F32),
            pltpu.SMEM((16,), jnp.int32),
            pltpu.VMEM((1, 256), jnp.int32),
            pltpu.VMEM((2, 16, 2, 8, 256), F32),
            pltpu.VMEM((2, 16, 2, 8, 256), F32),
            pltpu.VMEM((2, 16, 2, 8, 256), F32),
            pltpu.VMEM((4, 4, 3, 128, 256), F32),
            pltpu.VMEM((2, 128, 256), F32),
            pltpu.VMEM((4, 2, 3, 32, 256), F32),
            pltpu.VMEM((4, 2, 3, 32, 256), F32),
            pltpu.VMEM((2, 3, 16, 2, 2, 8, 256), F32),
            pltpu.VMEM((2, 2, 16, 8, 256), F32),
            pltpu.VMEM((3, 2, 128, 256), F32),
            pltpu.VMEM((256, 256), jnp.bfloat16),
            pltpu.VMEM((128, 128), F32),
            pltpu.VMEM((2, 32, 256), F32),
            pltpu.VMEM((2, 24, 8, 128), F32),
            pltpu.SMEM((16,), jnp.int32),
            dma((3,)),
            dma,
            dma((3,)),
            dma,
            dma((4, 2, 3)),
            dma((2,)),
            dma((4, 2, 3)),
            dma((2,)),
            dma((2,)),
            dma,
            dma((2, 2)),
        ],
        compiler_params=pltpu.CompilerParams(
            collective_id=0, has_side_effects=True, vmem_limit_bytes=40 * 1024 * 1024
        ),
    )(frequency, *[
        pltpu.with_memory_space_constraint(v, pltpu.HBM)
        for v in (slot_time, mirror_rows.reshape(1, 256), velocity.reshape(cut))
    ])
    orbit, defect, new = pl.pallas_call(
        finish,
        out_shape=shapes,
        in_specs=[vmem, vmem, hbm],
        out_specs=(hbm,) * 3,
        scratch_shapes=[pltpu.SMEM((1,), F32), dma((6,))],
        compiler_params=pltpu.CompilerParams(vmem_limit_bytes=4 * 1024 * 1024),
    )(*results)
    return orbit.reshape(velocity.shape), defect.reshape(velocity.shape), new


def solution(mesh):
    spread = P("inst", None, "space", None, None)
    return jax.shard_map(
        shards, mesh=mesh, in_specs=(spread, P(), P(), P()), out_specs=(spread, spread, P()),
        check_vma=False,
    )
```

```python
import functools
import math

import jax
import jax.numpy as jnp
from jax import lax
from jax.experimental import pallas as pl
from jax.experimental.pallas import tpu as pltpu
from jax.sharding import PartitionSpec as P

VISCOSITY = 0.5
DESCENT = 0.001
FREQUENCY_RATE = 0.025
MESH = pl.DeviceIdType.MESH
F32 = jnp.float32


def device(x, y, z, core):
    return ((y % 2) * 4 + z, x * 4 + (y // 2) * 2 + core)


def chip_of(j):
    y = j // 4
    r = j % 4
    return y, jnp.where(y % 2 == 0, r, 3 - r)


def weight(k):
    k = k % 16
    if k == 0:
        return 0.0
    angle = math.pi * k / 16
    return 0.5 * (-1.0) ** k * math.cos(angle) / math.sin(angle)


def kernel(
    freq_in, times_in, mirror_in, vel, orbit, defect, fout, freq, times, mirror,
    rbuf0, rbuf1, rbuf2, fld, orb, xsend, xrecv, obuf, mbuf, dbuf, mat, kmat, acc, drift, inv,
    small, in_send, in_recv, x_send, x_recv, y_send, y_recv, o_send, o_recv, d_send, d_recv,
):
    inst = lax.axis_index("inst")
    space = lax.axis_index("space")
    z = inst % 4
    yhi = space // 2 % 2
    y = yhi * 2 + inst // 4
    x = space // 4
    core = space % 2
    myj = y * 4 + jnp.where(y % 2 == 0, z, 3 - z)
    outs = (defect, orbit)
    rbuf = (rbuf0, rbuf1, rbuf2)

    barrier = pltpu.get_barrier_semaphore()

    steps = sorted(
        ((dy, dz, dc) for dy in range(4) for dz in range(4) for dc in range(2)),
        key=lambda d: -min(d[0], 4 - d[0]) - min(d[1], 4 - d[1]),
    )
    friends = [
        device(x, (y + dy) % 4, (z + dz) % 4, (core + dc) % 2)
        for dy, dz, dc in steps if dy + dz > 0
    ]
    friends += [device((x + 1 + k // 2) % 4, y, z, (core + k) % 2) for k in (2, 3, 0, 1, 4, 5)]
    friends += [device(x, y, z, 1 - core)]
    for friend in friends:
        pl.semaphore_signal(barrier, inc=1, device_id=friend, device_id_type=MESH)
    far = device((x + jnp.where(core == 1, 1, 3)) % 4, y, z, 1 - core)
    near = device(x, y, z, 1 - core)
    fetches = [
        pltpu.make_async_copy(src, dst, small.at[k])
        for k, (src, dst) in enumerate(
            ((freq_in, freq), (times_in, times), (mirror_in, mirror))
        )
    ]
    for copy in fetches:
        copy.start()
    pl.semaphore_wait(barrier, len(friends))

    def send_in(c):
        def body(k, carry):
            j = (k + myj) % 16
            cy, cz = chip_of(j)
            di, ds = device(x, cy, cz, yhi)
            src = vel.at[:, c, :, j]
            dst = rbuf[c].at[core, pl.ds(2 * inst, 2)]
            mine = (di == inst) & (ds == space)

            @pl.when(mine)
            def _():
                pltpu.make_async_copy(src, dst, in_recv.at[c]).start()

            @pl.when(jnp.logical_not(mine))
            def _():
                pltpu.make_async_remote_copy(
                    src, dst, in_send, in_recv.at[c], device_id=(di, ds), device_id_type=MESH
                ).start()

            return carry

        lax.fori_loop(0, 16, body, 0)

    for c in range(3):
        send_in(c)

    for copy in fetches:
        copy.wait()
    mat[...] = (
        lax.broadcasted_iota(jnp.int32, (256, 256), 0) == mirror[...]
    ).astype(F32).astype(jnp.bfloat16)
    rows = lax.broadcasted_iota(jnp.int32, (128, 128), 0)
    cols = lax.broadcasted_iota(jnp.int32, (128, 128), 1)
    gap = (rows // 8 - cols // 8 + 16) % 16
    table = jnp.zeros((128, 128), F32)
    for k in range(1, 16):
        table = jnp.where(gap == k, jnp.float32(weight(k)), table)
    kmat[...] = jnp.where(rows % 8 == cols % 8, table, 0.0)

    def invert(t, carry):
        def find(s, found):
            return jnp.where(times[s] == t, s, found)

        inv[t] = lax.fori_loop(0, 16, find, jnp.int32(0))
        return carry

    lax.fori_loop(0, 16, invert, 0)
    bottom = (x == 0) & (core == 0)
    top = (x == 3) & (core == 1)

    @pl.when(bottom)
    def _():
        fld[:, 0] = jnp.zeros((4, 3, 128, 256), F32)

    @pl.when(top)
    def _():
        fld[:, 3] = jnp.zeros((4, 3, 128, 256), F32)

    def reflect_z(v):
        high = v.astype(jnp.bfloat16)
        rest = v - high.astype(F32)
        middle = rest.astype(jnp.bfloat16)
        low = (rest - middle.astype(F32)).astype(jnp.bfloat16)
        m = mat[...]
        parts = [jnp.dot(u, m, preferred_element_type=F32) for u in (high, middle, low)]
        return parts[0] + (parts[1] + parts[2])

    def signed(c, v):
        return -v if c == 2 else v

    left = chip_of((myj + 15) % 16)
    right = chip_of((myj + 1) % 16)

    def send_planes(k, c, p):
        def planes(up, target):
            src, dst = (2, 0) if up else (1, 3)
            pltpu.make_async_remote_copy(
                fld.at[k, src, c], fld.at[k, dst, c], y_send.at[int(up)],
                y_recv.at[k, int(up), c], device_id=target, device_id_type=MESH,
            ).start()

        @pl.when(core == 1 - p)
        def _():
            planes(p == 1, near)

        @pl.when((core == p) & (x < 3 if p == 1 else x > 0))
        def _():
            planes(p == 1, far)

    def send_halo(k, c):
        for p in range(2):
            send_planes(k, c, p)
        send_rows(k, c)

    def send_rows(k, c):
        for p in range(2):
            part = pl.ds(16 * p, 16)
            tiles = fld[k, 1 + p, c].reshape(16, 8, 256)
            xsend[k, 0, c, part] = tiles[:, 0]
            xsend[k, 1, c, part] = tiles[:, 7]
        for side, wraps in ((0, myj == 0), (1, myj == 15)):

            @pl.when(wraps)
            def _():
                turned = signed(c, reflect_z(xsend[k, side, c]))
                for p in range(2):
                    xsend[k, side, c, pl.ds(16 * p, 8)] = turned[16 * p + 8 : 16 * p + 16]
                    xsend[k, side, c, pl.ds(16 * p + 8, 8)] = turned[16 * p : 16 * p + 8]

        for side, (cy, cz) in ((0, left), (1, right)):
            pltpu.make_async_remote_copy(
                xsend.at[k, side, c], xrecv.at[k, 1 - side, c], x_send,
                x_recv.at[k, 1 - side, c], device_id=device(x, cy, cz, core), device_id_type=MESH,
            ).start()

    def wait_for(ref, sem):
        pltpu.make_async_copy(ref, ref, sem).wait()

    def wait_halo(k, c):
        for side in range(2):
            wait_for(xrecv.at[k, side, c], x_recv.at[k, side, c])

        @pl.when(jnp.logical_not(bottom))
        def _():
            wait_for(fld.at[k, 0, c], y_recv.at[k, 1, c])

        @pl.when(jnp.logical_not(top))
        def _():
            wait_for(fld.at[k, 3, c], y_recv.at[k, 0, c])

    row = lax.broadcasted_iota(jnp.int32, (32, 256), 0) % 8

    def spread(v):
        return jnp.broadcast_to(v[:, None, :], (4, 8, 256)).reshape(32, 256)

    def speed_of(p):
        plane = (4 * x + 2 * core + p).astype(F32)
        return 2.0 * (plane + 0.5) / 16 - 1.0

    def inner(k, c, p, q, scale):
        part = pl.ds(q * 32, 32)
        v = fld[k, 1 + p, c, part]
        xm = jnp.where(row == 0, 0.0, pltpu.roll(v, 1, 0))
        xp = jnp.where(row == 7, 0.0, pltpu.roll(v, 31, 0))
        total = fld[k, 2 - p, c, part] + xm + xp
        total = total + pltpu.roll(v, 1, 1) + pltpu.roll(v, 255, 1) - 6.0 * v
        return part, scale * total + speed_of(p) * (0.5 * (xp - xm))

    def outer(k, c, p, q, scale):
        part = pl.ds(q * 32, 32)
        start = 16 * p
        edge = pl.ds(start if isinstance(p, int) else pl.multiple_of(start, 16), 16)
        half = 0.5 * speed_of(p)
        before = spread((scale - half) * xrecv[k, 0, c, edge][q * 4 : q * 4 + 4])
        after = spread((scale + half) * xrecv[k, 1, c, edge][q * 4 : q * 4 + 4])
        rows = jnp.where(row == 0, before, jnp.where(row == 7, after, 0.0))
        return part, scale * fld[k, 3 * p, c, part] + rows

    def tiles(body, after=None):
        def step(p, carry):
            for q in range(4):
                body(p, q)
            if after is not None:
                after(p)
            return carry

        if after is None:
            lax.fori_loop(0, 2, step, 0)
        else:
            for p in range(2):
                step(p, 0)

    def derive(k, c):
        for p in range(2):
            dbuf[c, p] = jnp.dot(
                kmat[...], fld[k, 1 + p, c], preferred_element_type=F32,
                precision=lax.Precision.HIGHEST,
            )

    def symmetrize(c):
        wait_for(rbuf[c], in_recv.at[c])

        def take(p, t, half):
            return rbuf[c][p, inv[t % 16], half]

        for p in range(2):
            other = jnp.concatenate([take(p, t + 8, 1) for t in range(16)], axis=0)
            own = jnp.concatenate([take(p, t, 0) for t in range(16)], axis=0)
            fld[0, 1 + p, c] = 0.5 * (own + signed(c, reflect_z(other)))
            send_planes(0, c, p)
        send_rows(0, c)

    def residual_inner(c, omega):
        derive(0, c)

        def body(p, q):
            part, value = inner(0, c, p, q, -VISCOSITY)
            fld[1, 1 + p, c, part] = omega * dbuf[c, p, part] + value

        tiles(body)

    def residual_outer(c):
        wait_halo(0, c)

        def body(p, q):
            part, value = outer(0, c, p, q, -VISCOSITY)
            value = fld[1, 1 + p, c, part] + value
            fld[1, 1 + p, c, part] = value
            acc[0] += value * dbuf[c, p, part]

        tiles(body)

    def prepare_inner(c):
        derive(2, c)

        def body(p, q):
            part, value = inner(2, c, p, q, -VISCOSITY)
            fld[3, 1 + p, c, part] = value

        tiles(body)

    def prepare_outer(c):
        wait_halo(2, c)

        def body(p, q):
            part, value = outer(2, c, p, q, -VISCOSITY)
            fld[3, 1 + p, c, part] += value

        tiles(body)

    def complete(c, omega):
        def body(p, q):
            part = pl.ds(q * 32, 32)
            d = dbuf[c, p, part]
            value = omega * d + fld[3, 1 + p, c, part]
            fld[3, 1 + p, c, part] = value
            acc[1] += value * d

        tiles(body)
        send_halo(3, c)

    def field_inner(k, c, omega):
        derive(k, c)

        def body(p, q):
            part, value = inner(k, c, p, q, VISCOSITY)
            dbuf[c, p, part] = omega * dbuf[c, p, part] + value

        tiles(body)

    def field_outer(k, c, store, after=None):
        wait_halo(k, c)

        def body(p, q):
            part, value = outer(k, c, p, q, VISCOSITY)
            rate = dbuf[c, p, part] + value
            store(p, part, fld[k - 1, 1 + p, c, part] + DESCENT * rate)

        tiles(body, after)

    def next_outer(c):
        def store(p, part, value):
            fld[2, 1 + p, c, part] = value

        field_outer(1, c, store, lambda p: send_planes(2, c, p))
        send_rows(2, c)

    stages = (
        (0, 16, y * 4 + z, lambda r: device(x, r // 4, r % 4, core)),
        (16, 8, x * 2 + core, lambda r: device(r // 2, y, z, r % 2)),
    )

    def drift_send(it, stage, tile):
        base, size, rank, of = stages[stage]
        drift[it, base + rank] = tile

        def body(k, carry):
            pltpu.make_async_remote_copy(
                drift.at[it, base + rank], drift.at[it, base + rank], d_send,
                d_recv.at[it, stage], device_id=of((rank + k) % size), device_id_type=MESH,
            ).start()
            return carry

        lax.fori_loop(1, size, body, 0)

    def drift_sum(it, stage):
        base, size, _, _ = stages[stage]
        wait_for(drift.at[it, pl.ds(base, size - 1)], d_recv.at[it, stage])
        tile = drift[it, base]
        for k in range(1, size):
            tile = tile + drift[it, base + k]
        return tile

    def drift_start(it):
        a = acc[it]
        tile = a[0:8] + a[8:16] + a[16:24] + a[24:32]
        drift_send(it, 0, tile[:, :128] + tile[:, 128:])

    entries = 16 * 3 * 16 * 256 * 256

    def drift_end(it, omega):
        return omega - FREQUENCY_RATE * (jnp.sum(drift_sum(it, 1)) / (entries // 2))

    def send_out(o, c, source):
        for p in range(2):
            value = source(p)[...]
            turned = signed(c, reflect_z(value)).reshape(16, 8, 256)
            mbuf[p, 0] = value.reshape(16, 8, 256)
            mbuf[p, 1, 0:8] = turned[8:16]
            mbuf[p, 1, 8:16] = turned[0:8]

            def build(i, carry):
                for s in range(2):
                    t = times[2 * i + s]
                    obuf[o, c, p * 8 + i, s, 0] = mbuf[p, 0, t]
                    obuf[o, c, p * 8 + i, s, 1] = mbuf[p, 1, t]
                return carry

            lax.fori_loop(0, 8, build, 0)

            def body(k, carry):
                di = (inst + 1 + k) % 8
                ds = x * 4 + core * 2 + p
                src = obuf.at[o, c, p * 8 + di]
                dst = outs[o].at[:, c, :, myj]
                mine = (di == inst) & (ds == space)

                @pl.when(mine)
                def _():
                    pltpu.make_async_copy(src, dst, o_recv.at[o]).start()

                @pl.when(jnp.logical_not(mine))
                def _():
                    pltpu.make_async_remote_copy(
                        src, dst, o_send.at[o], o_recv.at[o], device_id=(di, ds),
                        device_id_type=MESH,
                    ).start()

                return carry

            lax.fori_loop(0, 8, body, 0)

    acc[...] = jnp.zeros(acc.shape, F32)
    omega = freq[0]
    for c in range(3):
        symmetrize(c)
        residual_inner(c, omega)
    for c in range(3):
        residual_outer(c)
        if c == 2:
            drift_start(0)
        send_halo(1, c)
    for c in range(3):
        field_inner(1, c, omega)
    next_outer(0)
    drift_send(0, 1, drift_sum(0, 0))
    prepare_inner(0)
    next_outer(1)
    next_outer(2)
    prepare_outer(0)
    prepare_inner(1)
    prepare_inner(2)
    omega = drift_end(0, omega)
    for c in range(3):
        if c > 0:
            prepare_outer(c)
        complete(c, omega)
    drift_start(1)
    for c in range(3):
        send_out(0, c, lambda p: fld.at[3, 1 + p, c])
    for c in range(3):
        field_inner(3, c, omega)

        def keep(p, part, value):
            orb[p, part] = value

        field_outer(3, c, keep)
        send_out(1, c, lambda p: orb.at[p])
    drift_send(1, 1, drift_sum(1, 0))
    freq[0] = drift_end(1, omega)
    result = pltpu.make_async_copy(freq, fout, small.at[0])
    result.start()
    result.wait()

    for o in range(2):
        wait_for(outs[o], o_recv.at[o])
    part = pl.ds(0, 15)

    @pl.when(core == yhi)
    def _():
        wait_for(vel.at[:, :, :, part], in_send)
        for o in range(2):
            wait_for(obuf.at[o, :, part], o_send.at[o])

    @pl.when(core != yhi)
    def _():
        wait_for(vel, in_send)
        for o in range(2):
            wait_for(obuf.at[o], o_send.at[o])

    wait_for(xsend, x_send)

    @pl.when(jnp.logical_not(top))
    def _():
        wait_for(fld.at[:, 2], y_send.at[1])

    @pl.when(jnp.logical_not(bottom))
    def _():
        wait_for(fld.at[:, 1], y_send.at[0])

    wait_for(drift.at[:, pl.ds(0, 22)], d_send)


def finish(orbit, defect, new, orbit_out, defect_out, new_out, one, sems):
    first = pltpu.make_async_copy(new, one, sems.at[0])
    first.start()
    copies = [
        pltpu.make_async_copy(src.at[s], dst.at[s], sems.at[1 + 2 * k + s])
        for k, (src, dst) in enumerate(((orbit, orbit_out), (defect, defect_out)))
        for s in range(2)
    ]
    for copy in copies:
        copy.start()
    first.wait()
    copies.append(pltpu.make_async_copy(one, new_out, sems.at[5]))
    copies[-1].start()
    for copy in copies:
        copy.wait()


def shards(velocity, frequency, slot_time, mirror_rows):
    cut = (2, 3, 2, 16, 8, 256)
    whole = jax.ShapeDtypeStruct(cut, F32)
    shapes = (whole, whole, jax.ShapeDtypeStruct((1,), F32))
    hbm = pl.BlockSpec(memory_space=pltpu.HBM)
    vmem = pl.BlockSpec(memory_space=pltpu.VMEM)
    dma = pltpu.SemaphoreType.DMA
    results = pl.pallas_call(
        kernel,
        out_shape=(pltpu.VMEM(cut, F32), pltpu.VMEM(cut, F32), shapes[2]),
        in_specs=[hbm] * 4,
        out_specs=(vmem, vmem, hbm),
        scratch_shapes=[
            pltpu.SMEM((1,), F32),
            pltpu.SMEM((16,), jnp.int32),
            pltpu.VMEM((1, 256), jnp.int32),
            pltpu.VMEM((2, 16, 2, 8, 256), F32),
            pltpu.VMEM((2, 16, 2, 8, 256), F32),
            pltpu.VMEM((2, 16, 2, 8, 256), F32),
            pltpu.VMEM((4, 4, 3, 128, 256), F32),
            pltpu.VMEM((2, 128, 256), F32),
            pltpu.VMEM((4, 2, 3, 32, 256), F32),
            pltpu.VMEM((4, 2, 3, 32, 256), F32),
            pltpu.VMEM((2, 3, 16, 2, 2, 8, 256), F32),
            pltpu.VMEM((2, 2, 16, 8, 256), F32),
            pltpu.VMEM((3, 2, 128, 256), F32),
            pltpu.VMEM((256, 256), jnp.bfloat16),
            pltpu.VMEM((128, 128), F32),
            pltpu.VMEM((2, 32, 256), F32),
            pltpu.VMEM((2, 24, 8, 128), F32),
            pltpu.SMEM((16,), jnp.int32),
            dma((3,)),
            dma,
            dma((3,)),
            dma,
            dma((4, 2, 3)),
            dma((2,)),
            dma((4, 2, 3)),
            dma((2,)),
            dma((2,)),
            dma,
            dma((2, 2)),
        ],
        compiler_params=pltpu.CompilerParams(
            collective_id=0, has_side_effects=True, vmem_limit_bytes=40 * 1024 * 1024
        ),
    )(frequency, *[
        pltpu.with_memory_space_constraint(v, pltpu.HBM)
        for v in (slot_time, mirror_rows.reshape(1, 256), velocity.reshape(cut))
    ])
    orbit, defect, new = pl.pallas_call(
        finish,
        out_shape=shapes,
        in_specs=[vmem, vmem, hbm],
        out_specs=(hbm,) * 3,
        scratch_shapes=[pltpu.SMEM((1,), F32), dma((6,))],
        compiler_params=pltpu.CompilerParams(vmem_limit_bytes=4 * 1024 * 1024),
    )(*results)
    return orbit.reshape(velocity.shape), defect.reshape(velocity.shape), new


def solution(mesh):
    spread = P("inst", None, "space", None, None)
    return jax.shard_map(
        shards, mesh=mesh, in_specs=(spread, P(), P(), P()), out_specs=(spread, spread, P()),
        check_vma=False,
    )
```
